256 devices in a mesh: freq: 64 (over y, z, x_lo), rcv: 4 (over x_hi, core).
Axes of the slice: x: 4 (x_hi: 2, x_lo: 2; x = x_hi * 2 + x_lo), y: 4, z: 8, core: 2. Of those that a mesh axis runs over, the one named last changes fastest.
Arguments:
- traces: bfloat16 [128, 4096, 1024], P('freq', 'rcv'), may hold values from -0.75 to 0.75
- downgoing: bfloat16 [64, 2, 4096, 2048], P('freq', None, 'rcv'), may hold values from -4 to 4
Outputs:
- reflectivity: float32 [64, 2048, 2, 128], P('freq', 'rcv')
The draws below stay inside these ranges and needn't reach their ends.
All inputs are finite; a program needn't handle non-finite values.
Results may differ from the reference program's by a relative error of at most 0.0032.
Values may be sent and summed in bfloat16 or wider, within the bound.
A program may use at most 64 MiB of HBM per device.

```python
import math
import jax
import jax.numpy as jnp
from jax import lax

RECEIVERS = 4096
VSOURCES = 2048
SAMPLES = 1024
SHOTS = 128
ITERS = 2
FREQS = 64


def draw_downgoing(key, part):
    key = jax.random.fold_in(key, 7)
    key_base, key_row, key_col = jax.random.split(key, 3)
    shape = (FREQS, 2, RECEIVERS, VSOURCES)
    base = jnp.clip(jax.random.normal(key_base, shape, jnp.float32), -4.0, 4.0)
    row_span = math.log(10.0)
    row_scale = jnp.exp(jax.random.uniform(key_row, (FREQS, 1, RECEIVERS, 1), jnp.float32) * row_span)
    col_scale = jnp.exp(jax.random.uniform(key_col, (FREQS, 1, 1, VSOURCES), jnp.float32) * math.log(10.0))
    ramp = 3.0 ** (jnp.arange(FREQS, dtype=jnp.float32) / max(FREQS - 1, 1))
    values = base * row_scale * col_scale * ramp[:, None, None, None] / (4.0 * math.sqrt(VSOURCES))
    return jnp.clip(values, -4.0, 4.0).astype(jnp.bfloat16)


def shard_levels(own_key, extent, cuts, smallest, largest):
    gain, own = 1.0, jax.random.fold_in(own_key, 6)
    for dim, parts in cuts:
        steps = jnp.exp(jax.random.uniform(jax.random.fold_in(own, dim), (parts,), jnp.float32, smallest / len(cuts), largest / len(cuts)))
        gain = gain * jnp.repeat(steps, extent[dim] // parts).reshape([-1 if axis == dim else 1 for axis in range(len(extent))])
    return gain


def scatter_about(stream_key, dims, spread, bound, pieces=(), held_as=jnp.bfloat16):
    values = jax.random.normal(stream_key, dims, jnp.float32) * spread
    if len(pieces) > 0:
        values = shard_levels(stream_key, dims, pieces, -0.22, 0.18) * values
    return jnp.clip(values, min=-bound, max=bound).astype(held_as)


def setup_inputs(seed: int = 0) -> dict:
    arg_keys = jax.random.split(jax.random.key(seed), 3)
    return {
        "traces": scatter_about(arg_keys[0], (SHOTS, RECEIVERS, SAMPLES), 0.125, 0.75, ((0, 64), (1, 4))),
        "downgoing": draw_downgoing(jax.random.fold_in(arg_keys[2], 71), 0),
    }


epsilon = 1e-06

def spectrum_table(count_time, count_freq):
    times = jnp.arange(count_time, dtype=jnp.int32)
    bins = jnp.arange(count_freq, dtype=jnp.int32) + 1
    phase = (times[:, None] * bins[None, :] % count_time).astype(jnp.float32) * (2.0 * math.pi / count_time)
    return jnp.stack([jnp.cos(phase), -jnp.sin(phase)], axis=-1).reshape(count_time, 2 * count_freq)

def reference(traces, downgoing):
    shots, receivers, samples = traces.shape
    nfreq = downgoing.shape[0]
    vsources = downgoing.shape[3]
    table = spectrum_table(samples, nfreq)
    spectrum = jnp.dot(traces.astype(jnp.float32).reshape(shots * receivers, samples), table, precision=lax.Precision.HIGHEST).reshape(shots, receivers, nfreq, 2)
    spectrum = spectrum.transpose(2, 1, 3, 0)

    def forward(right_vec):
        rounded = lax.optimization_barrier(right_vec.astype(jnp.bfloat16))

        def one_freq(index):
            oper = lax.dynamic_index_in_dim(downgoing, index, 0, keepdims=False).astype(jnp.float32)
            vec = lax.dynamic_index_in_dim(rounded, index, 0, keepdims=False).astype(jnp.float32)
            prod = jnp.einsum('cnv,vm->cnm', oper, vec.reshape(vsources, 2 * shots), precision=lax.Precision.HIGHEST).reshape(2, receivers, 2, shots)
            real_part = prod[0, :, 0] - prod[1, :, 1]
            imag_part = prod[0, :, 1] + prod[1, :, 0]
            return jnp.stack([real_part, imag_part], axis=1)
        return lax.map(one_freq, jnp.arange(nfreq, dtype=jnp.int32))

    def adjoint(left_vec):
        rounded = lax.optimization_barrier(left_vec.astype(jnp.bfloat16))

        def one_freq(index):
            oper = lax.dynamic_index_in_dim(downgoing, index, 0, keepdims=False).astype(jnp.float32)
            vec = lax.dynamic_index_in_dim(rounded, index, 0, keepdims=False).astype(jnp.float32)
            prod = jnp.einsum('cnv,nm->cvm', oper, vec.reshape(receivers, 2 * shots), precision=lax.Precision.HIGHEST).reshape(2, vsources, 2, shots)
            real_part = prod[0, :, 0] + prod[1, :, 1]
            imag_part = prod[0, :, 1] - prod[1, :, 0]
            return jnp.stack([real_part, imag_part], axis=1)
        return lax.map(one_freq, jnp.arange(nfreq, dtype=jnp.int32))
    beta_now = jnp.sqrt(jnp.sum(spectrum * spectrum) + epsilon)
    left_vec = spectrum / beta_now
    right_vec = adjoint(left_vec)
    alpha_now = jnp.sqrt(jnp.sum(right_vec * right_vec) + epsilon)
    right_vec = right_vec / alpha_now
    search = right_vec
    solution = jnp.zeros_like(right_vec)
    phi_bar = beta_now
    rho_bar = alpha_now
    for step in range(ITERS):
        left_vec = forward(right_vec) - alpha_now * left_vec
        beta_now = jnp.sqrt(jnp.sum(left_vec * left_vec) + epsilon)
        left_vec = left_vec / beta_now
        right_vec = adjoint(left_vec) - beta_now * right_vec
        alpha_now = jnp.sqrt(jnp.sum(right_vec * right_vec) + epsilon)
        right_vec = right_vec / alpha_now
        rho_new = jnp.sqrt(rho_bar * rho_bar + beta_now * beta_now)
        cosine = rho_bar / rho_new
        sine_val = beta_now / rho_new
        theta_step = sine_val * alpha_now
        rho_bar = -cosine * alpha_now
        phi_step = cosine * phi_bar
        phi_bar = sine_val * phi_bar
        solution = solution + phi_step / rho_new * search
        search = right_vec - theta_step / rho_new * search
    return solution
```

```python
import functools
import math

import jax
import jax.numpy as jnp
import ml_dtypes
import numpy as np
from jax import lax
from jax.experimental import pallas as pl
from jax.experimental.pallas import tpu as pltpu
from jax.sharding import PartitionSpec as P

EPS = 1e-06
MESH = pl.DeviceIdType.MESH
BF16 = jnp.bfloat16
F32 = jnp.float32
FREQS = 64
RCV = 4
SAMPLES = 1024
ROWS = 1024
COLS = 2048
BLK = 512
M = 128
SIGMA = 2.0**-10
TAU = 2.0**-8


def dft_table():
    times = np.arange(SAMPLES, dtype=np.int64)
    bins = np.arange(FREQS, dtype=np.int64) + 1
    phase = (bins[:, None] * times[None, :] % SAMPLES).astype(np.float64) * (2.0 * math.pi / SAMPLES)
    table = np.concatenate([np.cos(phase), -np.sin(phase)], axis=0) * SIGMA
    high = table.astype(ml_dtypes.bfloat16)
    low = (table - high.astype(np.float64)).astype(ml_dtypes.bfloat16)
    return np.concatenate([high, low], axis=0)


def lane_sums(x):
    acc = x[:, 0:128]
    for t in range(1, x.shape[1] // 128):
        acc = acc + x[:, t * 128 : (t + 1) * 128]
    return jnp.sum(acc, axis=0, keepdims=True)


def nt_dot(a, b):
    return lax.dot_general(a, b, (((1,), (1,)), ((), ())), preferred_element_type=F32)


def kernel(
    table_ref, traces_ref, oper_ref, out_ref,
    tr, op, s32, f32s, sb, rb, xu, xy, ps, pr, cc, cs, cr, cl, clr, vop, vn, yy, zz, tmp,
    ar_src, ar1, ar_mid, ar2,
    tr_sem, op_sem, a_ss, a_rs, p_ss, p_rs, x_ss, x_rs, g_ss, g_rs, l_ss, l_rs, r_ss, r_rs,
):
    f = lax.axis_index("freq")
    r = lax.axis_index("rcv")
    h = r // 2
    e = lax.rem(r, 2)
    sib = (f, h * 2 + 1 - e)
    xp = (f, (1 - h) * 2 + e)
    g1 = lax.rem(f, 16)
    fy = f // 16
    g2 = fy * 4 + r

    def peer1(d):
        return (fy * 16 + lax.rem(g1 + d, 16), r)

    def peer2(d):
        q = lax.rem(g2 + d, 16)
        return ((q // 4) * 16 + g1, lax.rem(q, 4))

    def local(src, dst, sem):
        return pltpu.make_async_copy(src, dst, sem)

    def remote(src, dst, ss, rs, to):
        return pltpu.make_async_remote_copy(
            src_ref=src, dst_ref=dst, send_sem=ss, recv_sem=rs, device_id=to, device_id_type=MESH
        )

    tr_copies = [local(traces_ref.at[s], tr.at[s], tr_sem.at[s]) for s in range(2)]
    for c in tr_copies:
        c.start()
    op_copy = local(oper_ref, op, op_sem)
    op_copy.start()

    barrier = pltpu.get_barrier_semaphore()

    def greet(d, c):
        pl.semaphore_signal(
            barrier, inc=1, device_id=(lax.rem(f + d, FREQS), r), device_id_type=MESH
        )
        return c

    lax.fori_loop(1, FREQS, greet, 0)

    def greet2(d, c):
        to = (lax.rem(fy + d // 3, 4) * 16 + g1, lax.rem(r + 1 + lax.rem(d, 3), 4))
        pl.semaphore_signal(barrier, inc=1, device_id=to, device_id_type=MESH)
        return c

    lax.fori_loop(0, 12, greet2, 0)

    def dft(s):
        tr_copies[s].wait()
        for q in range(4):
            res = nt_dot(table_ref[...], tr[s, q * 256 : (q + 1) * 256, :])
            d = res[0:128] + res[128:256]
            for c in range(2):
                for qq in range(2):
                    s32[pl.ds((q * 2 + qq) * 2 + c, FREQS, stride=16), :] = d[
                        c * 64 : (c + 1) * 64, qq * 128 : (qq + 1) * 128
                    ]
        sb[s] = s32[...].astype(BF16).reshape(FREQS, 16, 128)

    def a2a_send(s):
        def go(d, c):
            to = lax.rem(f + d, FREQS)
            remote(sb.at[s, to], rb.at[s, f], a_ss.at[s], a_rs.at[s], (to, r)).start()
            return c

        lax.fori_loop(1, FREQS, go, 0)
        rb[s, f] = sb[s, f]

    def a2a_wait(ref, sem, s):
        part = ref.at[s, pl.ds(0, FREQS - 1)]
        local(part, part, sem.at[s]).wait()

    def relayout(s):
        f32s[...] = rb[s].astype(F32).reshape(FREQS * 16, 128)
        total = jnp.zeros((FREQS, 128), F32)
        for q in range(8):
            lo, hi = q * 128, (q + 1) * 128
            re = f32s[pl.ds(q * 2, FREQS, stride=16), :]
            im = f32s[pl.ds(q * 2 + 1, FREQS, stride=16), :]
            total = total + re * re + im * im
            reb, imb = re.astype(BF16), im.astype(BF16)
            xu[s, 0:64, lo:hi] = reb
            xu[s, 64:128, lo:hi] = imb
            xu[s, 0:64, ROWS + lo : ROWS + hi] = imb
            xu[s, 64:128, ROWS + lo : ROWS + hi] = -reb
        return jnp.sum(total, axis=0, keepdims=True)

    def cols(b):
        return pl.ds(pl.multiple_of(b * BLK, BLK), BLK)

    def sib_copy(k, s, i):
        return remote(ps.at[k, s, i], pr.at[k, s, i], p_ss.at[k, s, i], p_rs.at[k, s, i], sib)

    def x_copy(k, s, i):
        return remote(cs.at[k, s, i], cr.at[k, s, i], x_ss.at[k, s, i], x_rs.at[k, s, i], xp)

    def ag_copy(k, s, i, b):
        part = vop.at[k, s, :, cols(b)]
        return remote(part, part, g_ss.at[k, s, i], g_rs.at[k, s, i], sib)

    def lo_copy(s):
        return remote(cl.at[s, 1 - h], clr.at[s], l_ss.at[s], l_rs.at[s], xp)

    def adjoint(k, x, s):
        for i in range(2):
            ps[k, s, i] = jnp.dot(x[s], op[:, cols(2 * i + 1 - e)], preferred_element_type=F32)
            sib_copy(k, s, i).start()
        for i in range(2):
            p = jnp.dot(x[s], op[:, cols(2 * i + e)], preferred_element_type=F32)
            sib_copy(k, s, i).wait_recv()
            c = p + pr[k, s, i]
            cb = c.astype(BF16)
            cc[k, s, i] = c
            cs[k, s, i] = cb
            if k == 0:
                cl[s, i] = (c - cb.astype(F32)).astype(BF16)
            x_copy(k, s, i).start()

    def gather(k, s):
        for i in range(2):
            x_copy(k, s, i).wait_recv()
            v = cc[k, s, i] + cr[k, s, i].astype(F32)
            cc[k, s, i] = v
            vop[k, s, :, cols(2 * i + e)] = v.astype(BF16)
            ag_copy(k, s, i, 2 * i + e).start()
        for i in range(2):
            ag_copy(k, s, i, 2 * i + 1 - e).wait_recv()

    def forward(k, s, dst):
        vn[0:64] = -vop[k, s, 64:128]
        vn[64:128] = vop[k, s, 0:64]
        for n in range(2):
            lo, hi = n * 512, (n + 1) * 512
            dst[s, :, lo:hi] = nt_dot(vop[k, s], op[lo:hi, :]) + nt_dot(vn[...], op[ROWS + lo : ROWS + hi, :])

    def operand(s):
        y = (yy[s] * TAU).astype(BF16)
        xy[s, :, 0:ROWS] = y
        xy[s, 0:64, ROWS:] = y[64:128]
        xy[s, 64:128, ROWS:] = -y[0:64]

    def ar_start(n, tile):
        ar_src[n] = tile
        ar1[n, 0] = tile

        def go(d, c):
            remote(ar_src.at[n], ar1.at[n, d], r_ss.at[n, 0], r_rs.at[n, 0], peer1(d)).start()
            return c

        lax.fori_loop(1, 16, go, 0)

    def ar_wait(ref, n, sem):
        part = ref.at[n, pl.ds(1, 15)]
        local(part, part, sem).wait()

    def ar_middle(n):
        ar_wait(ar1, n, r_rs.at[n, 0])
        tile = jnp.sum(ar1[n], axis=0)
        ar_mid[n] = tile
        ar2[n, 0] = tile

        def go(d, c):
            remote(ar_mid.at[n], ar2.at[n, d], r_ss.at[n, 1], r_rs.at[n, 1], peer2(d)).start()
            return c

        lax.fori_loop(1, 16, go, 0)

    def ar_end(n):
        ar_wait(ar2, n, r_rs.at[n, 1])
        return jnp.sum(jnp.sum(ar2[n], axis=0), axis=1, keepdims=True)

    def tile_of(row0, row1=None):
        at = lax.broadcasted_iota(jnp.int32, (8, 128), 0)
        tile = jnp.where(at == 0, row0, 0.0)
        if row1 is not None:
            tile = jnp.where(at == 1, row1, tile)
        return tile

    dft(0)
    pl.semaphore_wait(barrier, FREQS - 1 + 12)
    a2a_send(0)
    dft(1)
    a2a_send(1)
    op_copy.wait()

    sum_u = jnp.zeros((1, 128), F32)
    for s in range(2):
        a2a_wait(rb, a_rs, s)
        sum_u = sum_u + relayout(s)
        adjoint(0, xu, s)

    sum_v = jnp.zeros((1, 128), F32)
    for s in range(2):
        gather(0, s)
        v = cc[0, s, h]
        sum_v = sum_v + lane_sums(v * v)
        if s == 1:
            ar_start(0, tile_of(sum_u, sum_v))
        forward(0, s, yy)
        operand(s)
        if s == 1:
            ar_middle(0)
        adjoint(1, xy, s)
    total = ar_end(0)
    beta0_sq = total[0:1] * (1.0 / SIGMA**2) + EPS
    beta0 = jnp.sqrt(beta0_sq)
    sb0 = beta0 * SIGMA
    alpha0_sq = total[1:2] / (sb0 * sb0) + EPS
    alpha0 = jnp.sqrt(alpha0_sq)
    g0 = sb0 * alpha0
    row = jnp.zeros((1, 128), F32)
    for s in range(2):
        left = yy[s] - alpha0_sq * xu[s, :, 0:ROWS].astype(F32)
        row = row + lane_sums(left * left)
    ar_start(1, tile_of(row))

    gather(1, 0)
    ar_middle(1)
    forward(1, 0, zz)
    total = ar_end(1)
    beta1_sq = total[0:1] / (g0 * g0) + EPS
    beta1 = jnp.sqrt(beta1_sq)
    k1 = (alpha0_sq + beta1_sq) * TAU
    gather(1, 1)
    row = jnp.zeros((1, 128), F32)
    for s in range(2):
        right = cc[1, s, h] - k1 * cc[0, s, h]
        row = row + lane_sums(right * right)
    ar_start(2, tile_of(row))
    for s in range(2):
        lo_copy(s).start()
    forward(1, 1, zz)
    ar_middle(2)
    total = ar_end(2)
    g1s = g0 * beta1 * TAU
    alpha1_sq = total[0:1] / (g1s * g1s) + EPS
    alpha1 = jnp.sqrt(alpha1_sq)
    row = jnp.zeros((1, 128), F32)
    ky = k1 + alpha1_sq * TAU
    ku = alpha1_sq * alpha0_sq * TAU
    for s in range(2):
        left = zz[s] - ky * yy[s] + ku * xu[s, :, 0:ROWS].astype(F32)
        row = row + lane_sums(left * left)
    ar_start(3, tile_of(row))
    for s in range(2):
        lo_copy(s).wait_recv()
    ar_middle(3)
    total = ar_end(3)
    g2s = g1s * alpha1
    beta2_sq = total[0:1] / (g2s * g2s) + EPS

    rho1_sq = alpha0_sq + beta1_sq
    rho1 = jnp.sqrt(rho1_sq)
    cos1 = alpha0 / rho1
    sin1 = beta1 / rho1
    theta1 = sin1 * alpha1
    rhobar = cos1 * alpha1
    phi1 = cos1 * beta0
    phibar = sin1 * beta0
    rho2 = jnp.sqrt(rhobar * rhobar + beta2_sq)
    phi2 = (rhobar / rho2) * phibar
    y2 = -(phi2 / rho2)
    c_v = (phi1 / rho1 - y2 * (theta1 / rho1)) / g0
    c_r = y2 / g2s
    for s in range(2):
        v = cc[0, s, h] + clr[s].astype(F32)
        right = cc[1, s, h] - k1 * v
        x = c_v * v + c_r * right
        for c in range(2):
            for t in range(4):
                tmp[t, pl.ds(c * 128 + s, 64, stride=2), :] = x[
                    c * 64 : (c + 1) * 64, t * 128 : (t + 1) * 128
                ]
    for c in range(2):
        for t in range(4):
            out_ref[pl.ds(t * 256 + c, 128, stride=2), :] = tmp[t, c * 128 : (c + 1) * 128, :].T

    for s in range(2):
        a2a_wait(sb, a_ss, s)
        lo_copy(s).wait_send()
        for k in range(2):
            for i in range(2):
                sib_copy(k, s, i).wait_send()
                x_copy(k, s, i).wait_send()
                ag_copy(k, s, i, 2 * i + e).wait_send()
    for n in range(4):
        ar_wait(ar1, n, r_ss.at[n, 0])
        ar_wait(ar2, n, r_ss.at[n, 1])


def per_device(table, traces, downgoing):
    vmem = pltpu.VMEM
    dma = pltpu.SemaphoreType.DMA
    scratch = [
        vmem((2, ROWS, SAMPLES), BF16),
        vmem((2 * ROWS, COLS), BF16),
        vmem((FREQS * 16, 128), F32),
        vmem((FREQS * 16, 128), F32),
        vmem((2, FREQS, 16, 128), BF16),
        vmem((2, FREQS, 16, 128), BF16),
        vmem((2, M, 2 * ROWS), BF16),
        vmem((2, M, 2 * ROWS), BF16),
        vmem((2, 2, 2, M, BLK), F32),
        vmem((2, 2, 2, M, BLK), F32),
        vmem((2, 2, 2, M, BLK), F32),
        vmem((2, 2, 2, M, BLK), BF16),
        vmem((2, 2, 2, M, BLK), BF16),
        vmem((2, 2, M, BLK), BF16),
        vmem((2, M, BLK), BF16),
        vmem((2, 2, M, COLS), BF16),
        vmem((M, COLS), BF16),
        vmem((2, M, ROWS), F32),
        vmem((2, M, ROWS), F32),
        vmem((4, 2 * M, 128), F32),
        vmem((4, 8, 128), F32),
        vmem((4, 16, 8, 128), F32),
        vmem((4, 8, 128), F32),
        vmem((4, 16, 8, 128), F32),
        dma((2,)), dma,
        dma((2,)), dma((2,)),
        dma((2, 2, 2)), dma((2, 2, 2)),
        dma((2, 2, 2)), dma((2, 2, 2)),
        dma((2, 2, 2)), dma((2, 2, 2)),
        dma((2,)), dma((2,)),
        dma((4, 2)), dma((4, 2)),
    ]
    out = pl.pallas_call(
        kernel,
        out_shape=jax.ShapeDtypeStruct((2 * BLK, 128), F32),
        in_specs=[
            pl.BlockSpec(memory_space=pltpu.VMEM),
            pl.BlockSpec(memory_space=pl.ANY),
            pl.BlockSpec(memory_space=pl.ANY),
        ],
        out_specs=pl.BlockSpec(memory_space=pltpu.VMEM),
        scratch_shapes=scratch,
        compiler_params=pltpu.CompilerParams(
            collective_id=0, has_side_effects=True, vmem_limit_bytes=52 * 2**20
        ),
        name="lsqr",
    )(table, traces, downgoing.reshape(2 * ROWS, COLS))
    return out.reshape(1, BLK, 2, 128)


def solution(mesh):
    table = dft_table()
    return jax.shard_map(
        lambda traces, downgoing: per_device(jnp.asarray(table), traces, downgoing),
        mesh=mesh,
        in_specs=(P("freq", "rcv", None), P("freq", None, "rcv", None)),
        out_specs=P("freq", "rcv", None, None),
        check_vma=False,
    )
```

```python
import math

import jax
import jax.numpy as jnp
import ml_dtypes
import numpy as np
from jax import lax
from jax.experimental import pallas as pl
from jax.experimental.pallas import tpu as pltpu
from jax.sharding import PartitionSpec as P

EPS = 1e-06
MESH = pl.DeviceIdType.MESH
BF16 = jnp.bfloat16
F32 = jnp.float32
FREQS = 64
RCV = 4
SAMPLES = 1024
ROWS = 1024
COLS = 2048
BLK = 512
M = 128
SIGMA = 2.0**-10
FAR_FIRST = (4, 3, 5, 2, 6, 1, 7, 0)
AR_NEAR = (8, 9, 7, 6, 10, 5, 11, 4, 12, 3, 13, 2, 14, 1, 15)
AR_FAR = (10, 9, 11, 8, 6, 14, 5, 7, 13, 15, 2, 4, 12, 1, 3)
TAU = 2.0**-8


def dft_table():
    times = np.arange(SAMPLES, dtype=np.int64)
    bins = np.arange(FREQS, dtype=np.int64) + 1
    phase = (bins[:, None] * times[None, :] % SAMPLES).astype(np.float64) * (2.0 * math.pi / SAMPLES)
    table = np.concatenate([np.cos(phase), -np.sin(phase)], axis=0) * SIGMA
    high = table.astype(ml_dtypes.bfloat16)
    low = (table - high.astype(np.float64)).astype(ml_dtypes.bfloat16)
    return np.concatenate([high, low], axis=0)


def lane_sums(x):
    acc = x[:, 0:128]
    for t in range(1, x.shape[1] // 128):
        acc = acc + x[:, t * 128 : (t + 1) * 128]
    return jnp.sum(acc, axis=0, keepdims=True)


def nt_dot(a, b):
    return lax.dot_general(a, b, (((1,), (1,)), ((), ())), preferred_element_type=F32)


def kernel(
    table_ref, traces_ref, oper_ref, out_ref,
    tb, tr, op, s32, f32s, sb, rb, xu, xy, ps, pr, cc, cs, cr, cl, clr, vop, xc, eye, ot, yy, zz, tmp,
    ar_src, ar1, ar_mid, ar2,
    tb_sem, tr_sem, op_sem, a_ss, a_rs, p_ss, p_rs, x_ss, x_rs, g_ss, g_rs, l_ss, l_rs, r_ss, r_rs,
):
    f = lax.axis_index("freq")
    r = lax.axis_index("rcv")
    h = r // 2
    e = lax.rem(r, 2)
    sib = (f, h * 2 + 1 - e)
    xp = (f, (1 - h) * 2 + e)
    g1 = lax.rem(f, 16)
    fy = f // 16
    fz = g1 // 2
    fl = lax.rem(f, 2)

    def peer1(d):
        return (fy * 16 + lax.rem(g1 + d, 16), r)

    def peer2(d):
        return (lax.rem(fy + d // 4, 4) * 16 + g1, lax.rem(r + lax.rem(d, 4), 4))

    def local(src, dst, sem):
        return pltpu.make_async_copy(src, dst, sem)

    def remote(src, dst, ss, rs, to):
        return pltpu.make_async_remote_copy(
            src_ref=src, dst_ref=dst, send_sem=ss, recv_sem=rs, device_id=to, device_id_type=MESH
        )

    flying = {}

    def launch(key, copy):
        copy.start()
        flying[key, "send"] = copy.wait_send
        flying[key, "recv"] = copy.wait_recv

    def land(*key):
        flying.pop((key, "recv"))()

    tb_copy = local(table_ref, tb, tb_sem)
    tb_copy.start()
    flying[("tb",), "recv"] = tb_copy.wait
    tr_copies = [local(traces_ref.at[s], tr.at[s], tr_sem.at[s]) for s in range(2)]
    for s in range(2):
        tr_copies[s].start()
        flying[("tr", s), "recv"] = tr_copies[s].wait

    barrier = pltpu.get_barrier_semaphore()

    def each_freq_peer(act):
        for dz in FAR_FIRST:

            def go(q, c, dz=dz):
                y = lax.rem(fy + q // 2, 4)
                z = lax.rem(fz + dz, 8)
                lo = lax.rem(fl + lax.rem(q, 2), 2)
                act(y * 16 + z * 2 + lo)
                return c

            lax.fori_loop(1 if dz == 0 else 0, 8, go, 0)

    def greet2(d, c):
        to = (lax.rem(fy + d // 3, 4) * 16 + g1, lax.rem(r + 1 + lax.rem(d, 3), 4))
        pl.semaphore_signal(barrier, inc=1, device_id=to, device_id_type=MESH)
        return c

    def greet(to):
        pl.semaphore_signal(barrier, inc=1, device_id=(to, r), device_id_type=MESH)

    lax.fori_loop(0, 12, greet2, 0)
    each_freq_peer(greet)

    op_copy = local(oper_ref, op, op_sem)
    op_copy.start()
    flying[("op",), "recv"] = op_copy.wait

    def dft(s):
        land("tr", s)
        for q in range(4):
            res = nt_dot(tb[...], tr[s, q * 256 : (q + 1) * 256, :])
            d = res[0:128] + res[128:256]
            for c in range(2):
                for qq in range(2):
                    s32[pl.ds((q * 2 + qq) * 2 + c, FREQS, stride=16), :] = d[
                        c * 64 : (c + 1) * 64, qq * 128 : (qq + 1) * 128
                    ]
        sb[:, s * 16 : (s + 1) * 16, :] = s32[...].astype(BF16).reshape(FREQS, 16, 128)

    def a2a_send(s):
        def go(to):
            part = pl.ds(s * 16, 16)
            remote(sb.at[to, part], rb.at[f, part], a_ss.at[s], a_rs.at[s], (to, r)).start()

        each_freq_peer(go)
        rb[f, s * 16 : (s + 1) * 16] = sb[f, s * 16 : (s + 1) * 16]
        most = (pl.ds(0, FREQS - 1), pl.ds(s * 16, 16))
        sent, got = sb.at[most], rb.at[most]
        flying[("a2a", s), "send"] = local(sent, sent, a_ss.at[s]).wait
        flying[("a2a", s), "recv"] = local(got, got, a_rs.at[s]).wait

    def relayout(s):
        f32s[...] = rb[:, s * 16 : (s + 1) * 16, :].astype(F32).reshape(FREQS * 16, 128)
        total = jnp.zeros((FREQS, 128), F32)
        for q in range(8):
            lo, hi = q * 128, (q + 1) * 128
            re = f32s[pl.ds(q * 2, FREQS, stride=16), :]
            im = f32s[pl.ds(q * 2 + 1, FREQS, stride=16), :]
            total = total + re * re + im * im
            reb, imb = re.astype(BF16), im.astype(BF16)
            xu[s, 0:64, lo:hi] = reb
            xu[s, 64:128, lo:hi] = imb
            xu[s, 0:64, ROWS + lo : ROWS + hi] = imb
            xu[s, 64:128, ROWS + lo : ROWS + hi] = -reb
        return jnp.sum(total, axis=0, keepdims=True)

    def cols(b):
        return pl.ds(pl.multiple_of(b * BLK, BLK), BLK)

    def sib_copy(k, s, i):
        return remote(ps.at[k, s, i], pr.at[k, s, i], p_ss.at[k, s, i], p_rs.at[k, s, i], sib)

    def x_copy(k, s, i):
        return remote(cs.at[k, s, i], cr.at[k, s, i], x_ss.at[k, s, i], x_rs.at[k, s, i], xp)

    def ag_copy(k, s, i, b):
        part = vop.at[k, s, b]
        return remote(part, part, g_ss.at[k, s, i], g_rs.at[k, s, i], sib)

    def lo_copy(s):
        return remote(cl.at[s, 1 - h], clr.at[s], l_ss.at[s], l_rs.at[s], xp)

    def adjoint(k, x, s):
        for i in range(2):
            ps[k, s, i] = jnp.dot(x[s], op[:, cols(2 * i + 1 - e)], preferred_element_type=F32)
            launch(("sib", k, s, i), sib_copy(k, s, i))
        for i in range(2):
            p = jnp.dot(x[s], op[:, cols(2 * i + e)], preferred_element_type=F32)
            land("sib", k, s, i)
            c = p + pr[k, s, i]
            cb = c.astype(BF16)
            cc[k, s, i] = c
            cs[k, s, i] = cb
            if k == 0:
                cl[s, i] = (c - cb.astype(F32)).astype(BF16)
            launch(("x", k, s, i), x_copy(k, s, i))

    def gather(k, s, i):
        land("x", k, s, i)
        v = cc[k, s, i] + cr[k, s, i].astype(F32)
        cc[k, s, i] = v
        vop[k, s, 2 * i + e] = v.astype(BF16)
        launch(("ag", k, s, i), ag_copy(k, s, i, 2 * i + e))

    def transpose_operator():
        at = [lax.broadcasted_iota(jnp.int32, (256, 256), d) for d in range(2)]
        eye[...] = jnp.where(at[0] == at[1], 1.0, 0.0).astype(BF16)

        def go(b, c):
            for q in range(2):
                for part in range(2):
                    for n in range(2):
                        rows = slice(part * ROWS + n * 512, part * ROWS + (n + 1) * 512)
                        col = pl.multiple_of(b * BLK + q * 256, 256)
                        ot[b, part * BLK + q * 256 : part * BLK + (q + 1) * 256, n * 512 : (n + 1) * 512] = nt_dot(
                            eye[...], op[rows, pl.ds(col, 256)]
                        ).astype(BF16)
            return c

        lax.fori_loop(0, 4, go, 0)

    def forward_block(k, s, b, dst, first):
        v = vop[k, s, b]
        xc[:, 0:BLK] = v
        xc[0:64, BLK:] = -v[64:128]
        xc[64:128, BLK:] = v[0:64]
        for n in range(2):
            lo, hi = n * 512, (n + 1) * 512
            part = jnp.dot(xc[...], ot[b, :, lo:hi], preferred_element_type=F32)
            if first:
                dst[s, :, lo:hi] = part
            else:
                dst[s, :, lo:hi] += part

    def forward(k, s, i, dst):
        forward_block(k, s, 2 * i + e, dst, i == 0)
        land("ag", k, s, i)
        forward_block(k, s, 2 * i + 1 - e, dst, False)

    def operand(s):
        y = (yy[s] * TAU).astype(BF16)
        xy[s, :, 0:ROWS] = y
        xy[s, 0:64, ROWS:] = y[64:128]
        xy[s, 64:128, ROWS:] = -y[0:64]

    def ar_start(n, tile):
        ar_src[n] = tile
        ar1[n, 0] = tile

        for d in AR_NEAR:
            remote(ar_src.at[n], ar1.at[n, d], r_ss.at[n, 0], r_rs.at[n, 0], peer1(d)).start()
        ar_flying(n, 0, ar1)

    def ar_flying(n, stage, ref):
        part = ref.at[n, pl.ds(1, 15)]
        flying[("ar", n, stage), "send"] = local(part, part, r_ss.at[n, stage]).wait
        flying[("ar", n, stage), "recv"] = local(part, part, r_rs.at[n, stage]).wait

    def ar_middle(n):
        land("ar", n, 0)
        tile = jnp.sum(ar1[n], axis=0)
        ar_mid[n] = tile
        ar2[n, 0] = tile

        for d in AR_FAR:
            remote(ar_mid.at[n], ar2.at[n, d], r_ss.at[n, 1], r_rs.at[n, 1], peer2(d)).start()
        ar_flying(n, 1, ar2)

    def ar_end(n):
        land("ar", n, 1)
        return jnp.sum(jnp.sum(ar2[n], axis=0), axis=1, keepdims=True)

    def tile_of(rows):
        at = lax.broadcasted_iota(jnp.int32, (8, 128), 0)
        tile = jnp.zeros((8, 128), F32)
        for i, row in enumerate(rows):
            tile = jnp.where(at == i, row, tile)
        return tile

    def body():
        land("tb")
        dft(0)
        dft(1)
        pl.semaphore_wait(barrier, FREQS - 1 + 12)
        a2a_send(0)
        a2a_send(1)
        land("op")
        transpose_operator()

        zero = jnp.zeros((1, 128), F32)
        sum_u = zero
        for s in range(2):
            land("a2a", s)
            sum_u = sum_u + relayout(s)
            adjoint(0, xu, s)

        sum_v, sum_y, sum_yu = zero, zero, zero
        for s in range(2):
            for i in range(2):
                gather(0, s, i)
                forward(0, s, i, yy)
            if s == 0:
                operand(s)
                adjoint(1, xy, s)
            v = cc[0, s, h]
            sum_v = sum_v + lane_sums(v * v)
            sum_y = sum_y + lane_sums(yy[s] * yy[s])
            sum_yu = sum_yu + lane_sums(yy[s] * xu[s, :, 0:ROWS].astype(F32))
        ar_start(0, tile_of([sum_u, sum_v, sum_y, sum_yu]))
        operand(1)
        adjoint(1, xy, 1)

        gather(1, 0, 0)
        forward(1, 0, 0, zz)
        ar_middle(0)
        gather(1, 0, 1)
        forward(1, 0, 1, zz)

        total = ar_end(0)
        s_u, s_v, s_y, s_yu = (total[i : i + 1] for i in range(4))
        beta0 = jnp.sqrt(s_u * (1.0 / SIGMA**2) + EPS)
        sb0 = beta0 * SIGMA
        alpha0_sq = s_v / (sb0 * sb0) + EPS
        alpha0 = jnp.sqrt(alpha0_sq)
        g0 = sb0 * alpha0
        s_left = jnp.maximum(s_y - alpha0_sq * (2.0 * s_yu - alpha0_sq * s_u), 0.0)
        beta1_sq = s_left / (g0 * g0) + EPS
        beta1 = jnp.sqrt(beta1_sq)
        k1 = (alpha0_sq + beta1_sq) * TAU

        sum_r, sum_g, sum_gl = zero, zero, zero
        for s in range(2):
            if s == 1:
                gather(1, 1, 0)
                forward(1, 1, 0, zz)
                gather(1, 1, 1)
                for t in range(2):
                    launch(("lo", t), lo_copy(t))
                forward(1, 1, 1, zz)
            right = cc[1, s, h] - k1 * cc[0, s, h]
            sum_r = sum_r + lane_sums(right * right)
            y = yy[s]
            left = y - alpha0_sq * xu[s, :, 0:ROWS].astype(F32)
            ahead = zz[s] - k1 * y
            sum_g = sum_g + lane_sums(ahead * ahead)
            sum_gl = sum_gl + lane_sums(ahead * left)
        ar_start(1, tile_of([sum_r, sum_g, sum_gl]))
        for s in range(2):
            land("lo", s)
        ar_middle(1)
        total = ar_end(1)
        s_r, s_g, s_gl = (total[i : i + 1] for i in range(3))
        g1s = g0 * beta1 * TAU
        alpha1_sq = s_r / (g1s * g1s) + EPS
        alpha1 = jnp.sqrt(alpha1_sq)
        g2s = g1s * alpha1
        a_sq = alpha1_sq * TAU
        s_left2 = jnp.maximum(s_g - a_sq * (2.0 * s_gl - a_sq * s_left), 0.0)
        beta2_sq = s_left2 / (g2s * g2s) + EPS

        rho1_sq = alpha0_sq + beta1_sq
        rho1 = jnp.sqrt(rho1_sq)
        cos1 = alpha0 / rho1
        sin1 = beta1 / rho1
        theta1 = sin1 * alpha1
        rhobar = cos1 * alpha1
        phi1 = cos1 * beta0
        phibar = sin1 * beta0
        rho2 = jnp.sqrt(rhobar * rhobar + beta2_sq)
        phi2 = (rhobar / rho2) * phibar
        y2 = -(phi2 / rho2)
        c_v = (phi1 / rho1 - y2 * (theta1 / rho1)) / g0
        c_r = y2 / g2s
        for s in range(2):
            v = cc[0, s, h] + clr[s].astype(F32)
            right = cc[1, s, h] - k1 * v
            x = c_v * v + c_r * right
            for c in range(2):
                for t in range(4):
                    tmp[t, pl.ds(c * 128 + s, 64, stride=2), :] = x[
                        c * 64 : (c + 1) * 64, t * 128 : (t + 1) * 128
                    ]
        for c in range(2):
            for t in range(4):
                out_ref[pl.ds(t * 256 + c, 128, stride=2), :] = tmp[t, c * 128 : (c + 1) * 128, :].T

    body()
    for wait in flying.values():
        wait()


def per_device(table, traces, downgoing):
    vmem = pltpu.VMEM
    dma = pltpu.SemaphoreType.DMA
    scratch = [
        vmem((4 * FREQS, SAMPLES), BF16),
        vmem((2, ROWS, SAMPLES), BF16),
        vmem((2 * ROWS, COLS), BF16),
        vmem((FREQS * 16, 128), F32),
        vmem((FREQS * 16, 128), F32),
        vmem((FREQS, 32, 128), BF16),
        vmem((FREQS, 32, 128), BF16),
        vmem((2, M, 2 * ROWS), BF16),
        vmem((2, M, 2 * ROWS), BF16),
        vmem((2, 2, 2, M, BLK), F32),
        vmem((2, 2, 2, M, BLK), F32),
        vmem((2, 2, 2, M, BLK), F32),
        vmem((2, 2, 2, M, BLK), BF16),
        vmem((2, 2, 2, M, BLK), BF16),
        vmem((2, 2, M, BLK), BF16),
        vmem((2, M, BLK), BF16),
        vmem((2, 2, 4, M, BLK), BF16),
        vmem((M, 2 * BLK), BF16),
        vmem((256, 256), BF16),
        vmem((4, 2 * BLK, ROWS), BF16),
        vmem((2, M, ROWS), F32),
        vmem((2, M, ROWS), F32),
        vmem((4, 2 * M, 128), F32),
        vmem((2, 8, 128), F32),
        vmem((2, 16, 8, 128), F32),
        vmem((2, 8, 128), F32),
        vmem((2, 16, 8, 128), F32),
        dma, dma((2,)), dma,
        dma((2,)), dma((2,)),
        dma((2, 2, 2)), dma((2, 2, 2)),
        dma((2, 2, 2)), dma((2, 2, 2)),
        dma((2, 2, 2)), dma((2, 2, 2)),
        dma((2,)), dma((2,)),
        dma((2, 2)), dma((2, 2)),
    ]
    out = pl.pallas_call(
        kernel,
        out_shape=jax.ShapeDtypeStruct((2 * BLK, 128), F32),
        in_specs=[
            pl.BlockSpec(memory_space=pl.ANY),
            pl.BlockSpec(memory_space=pl.ANY),
            pl.BlockSpec(memory_space=pl.ANY),
        ],
        out_specs=pl.BlockSpec(memory_space=pltpu.VMEM),
        scratch_shapes=scratch,
        compiler_params=pltpu.CompilerParams(
            collective_id=0, has_side_effects=True, vmem_limit_bytes=63 * 2**20
        ),
        name="lsqr",
    )(table, traces, downgoing.reshape(2 * ROWS, COLS))
    return out.reshape(1, BLK, 2, 128)


def solution(mesh):
    table = dft_table()
    return jax.shard_map(
        lambda traces, downgoing: per_device(jnp.asarray(table), traces, downgoing),
        mesh=mesh,
        in_specs=(P("freq", "rcv", None), P("freq", None, "rcv", None)),
        out_specs=P("freq", "rcv", None, None),
        check_vma=False,
    )
```

```python
import math

import jax
import jax.numpy as jnp
import ml_dtypes
import numpy as np
from jax import lax
from jax.experimental import pallas as pl
from jax.experimental.pallas import tpu as pltpu
from jax.sharding import PartitionSpec as P

EPS = 1e-06
MESH = pl.DeviceIdType.MESH
BF16 = jnp.bfloat16
F32 = jnp.float32
FREQS = 64
RCV = 4
SAMPLES = 1024
ROWS = 1024
COLS = 2048
BLK = 512
M = 128
SIGMA = 2.0**-10
FAR_FIRST = (4, 3, 5, 2, 6, 1, 7, 0)
AR_NEAR = (8, 9, 7, 6, 10, 5, 11, 4, 12, 3, 13, 2, 14, 1, 15)
AR_FAR = (10, 9, 11, 8, 6, 14, 5, 7, 13, 15, 2, 4, 12, 1, 3)
TAU = 2.0**-8


def dft_table():
    times = np.arange(SAMPLES, dtype=np.int64)
    bins = np.arange(FREQS, dtype=np.int64) + 1
    phase = (bins[:, None] * times[None, :] % SAMPLES).astype(np.float64) * (2.0 * math.pi / SAMPLES)
    table = np.concatenate([np.cos(phase), -np.sin(phase)], axis=0) * SIGMA
    high = table.astype(ml_dtypes.bfloat16)
    low = (table - high.astype(np.float64)).astype(ml_dtypes.bfloat16)
    return np.concatenate([high, low], axis=0)


def lane_sums(x):
    acc = x[:, 0:128]
    for t in range(1, x.shape[1] // 128):
        acc = acc + x[:, t * 128 : (t + 1) * 128]
    return jnp.sum(acc, axis=0, keepdims=True)


def nt_dot(a, b):
    return lax.dot_general(a, b, (((1,), (1,)), ((), ())), preferred_element_type=F32)


def kernel(
    table_ref, traces_ref, oper_ref, out_ref,
    tb, tr, op, s32, f32s, sb, rb, xu, xy, ps, pr, cc, cs, cr, cl, clr, vop, xc, eye, ot, yy, zz, tmp,
    ar_src, ar1, ar_mid, ar2,
    tb_sem, tr_sem, op_sem, a_ss, a_rs, p_ss, p_rs, x_ss, x_rs, g_ss, g_rs, l_ss, l_rs, r_ss, r_rs,
):
    f = lax.axis_index("freq")
    r = lax.axis_index("rcv")
    h = r // 2
    e = lax.rem(r, 2)
    sib = (f, h * 2 + 1 - e)
    xp = (f, (1 - h) * 2 + e)
    g1 = lax.rem(f, 16)
    fy = f // 16
    fz = g1 // 2
    fl = lax.rem(f, 2)

    def peer1(d):
        return (fy * 16 + lax.rem(g1 + d, 16), r)

    def peer2(d):
        return (lax.rem(fy + d // 4, 4) * 16 + g1, lax.rem(r + lax.rem(d, 4), 4))

    def local(src, dst, sem):
        return pltpu.make_async_copy(src, dst, sem)

    def remote(src, dst, ss, rs, to):
        return pltpu.make_async_remote_copy(
            src_ref=src, dst_ref=dst, send_sem=ss, recv_sem=rs, device_id=to, device_id_type=MESH
        )

    flying = {}

    def launch(key, copy):
        copy.start()
        flying[key, "send"] = copy.wait_send
        flying[key, "recv"] = copy.wait_recv

    def land(*key):
        flying.pop((key, "recv"))()

    tb_copy = local(table_ref, tb, tb_sem)
    tb_copy.start()
    flying[("tb",), "recv"] = tb_copy.wait
    tr_copies = [local(traces_ref.at[s], tr.at[s], tr_sem.at[s]) for s in range(2)]
    for s in range(2):
        tr_copies[s].start()
        flying[("tr", s), "recv"] = tr_copies[s].wait

    barrier = pltpu.get_barrier_semaphore()

    def each_freq_peer(act):
        for dz in FAR_FIRST:

            def go(q, c, dz=dz):
                y = lax.rem(fy + q // 2, 4)
                z = lax.rem(fz + dz, 8)
                lo = lax.rem(fl + lax.rem(q, 2), 2)
                act(y * 16 + z * 2 + lo)
                return c

            lax.fori_loop(1 if dz == 0 else 0, 8, go, 0)

    def greet2(d, c):
        to = (lax.rem(fy + d // 3, 4) * 16 + g1, lax.rem(r + 1 + lax.rem(d, 3), 4))
        pl.semaphore_signal(barrier, inc=1, device_id=to, device_id_type=MESH)
        return c

    def greet(to):
        pl.semaphore_signal(barrier, inc=1, device_id=(to, r), device_id_type=MESH)

    lax.fori_loop(0, 12, greet2, 0)
    each_freq_peer(greet)

    op_copy = local(oper_ref, op, op_sem)
    op_copy.start()
    flying[("op",), "recv"] = op_copy.wait

    def dft(s):
        land("tr", s)
        for q in range(4):
            res = nt_dot(tb[...], tr[s, q * 256 : (q + 1) * 256, :])
            d = res[0:128] + res[128:256]
            for c in range(2):
                for qq in range(2):
                    s32[pl.ds((q * 2 + qq) * 2 + c, FREQS, stride=16), :] = d[
                        c * 64 : (c + 1) * 64, qq * 128 : (qq + 1) * 128
                    ]
        sb[:, s * 16 : (s + 1) * 16, :] = s32[...].astype(BF16).reshape(FREQS, 16, 128)

    def a2a_send(s):
        def go(to):
            part = pl.ds(s * 16, 16)
            remote(sb.at[to, part], rb.at[f, part], a_ss.at[s], a_rs.at[s], (to, r)).start()

        each_freq_peer(go)
        rb[f, s * 16 : (s + 1) * 16] = sb[f, s * 16 : (s + 1) * 16]
        most = (pl.ds(0, FREQS - 1), pl.ds(s * 16, 16))
        sent, got = sb.at[most], rb.at[most]
        flying[("a2a", s), "send"] = local(sent, sent, a_ss.at[s]).wait
        flying[("a2a", s), "recv"] = local(got, got, a_rs.at[s]).wait

    def relayout(s):
        f32s[...] = rb[:, s * 16 : (s + 1) * 16, :].astype(F32).reshape(FREQS * 16, 128)
        total = jnp.zeros((FREQS, 128), F32)
        for q in range(8):
            lo, hi = q * 128, (q + 1) * 128
            re = f32s[pl.ds(q * 2, FREQS, stride=16), :]
            im = f32s[pl.ds(q * 2 + 1, FREQS, stride=16), :]
            total = total + re * re + im * im
            reb, imb = re.astype(BF16), im.astype(BF16)
            xu[s, 0:64, lo:hi] = reb
            xu[s, 64:128, lo:hi] = imb
            xu[s, 0:64, ROWS + lo : ROWS + hi] = imb
            xu[s, 64:128, ROWS + lo : ROWS + hi] = -reb
        return jnp.sum(total, axis=0, keepdims=True)

    def cols(b):
        return pl.ds(pl.multiple_of(b * BLK, BLK), BLK)

    def sib_copy(k, s, i):
        return remote(ps.at[k, s, i], pr.at[k, s, i], p_ss.at[k, s, i], p_rs.at[k, s, i], sib)

    def x_copy(k, s, i):
        return remote(cs.at[k, s, i], cr.at[k, s, i], x_ss.at[k, s, i], x_rs.at[k, s, i], xp)

    def ag_copy(k, s, i, b):
        part = vop.at[k, s, b]
        return remote(part, part, g_ss.at[k, s, i], g_rs.at[k, s, i], sib)

    def lo_copy(s):
        return remote(cl.at[s, 1 - h], clr.at[s], l_ss.at[s], l_rs.at[s], xp)

    def adjoint(k, x, s):
        for i in range(2):
            ps[k, s, i] = jnp.dot(x[s], op[:, cols(2 * i + 1 - e)], preferred_element_type=F32)
            launch(("sib", k, s, i), sib_copy(k, s, i))
        for i in range(2):
            p = jnp.dot(x[s], op[:, cols(2 * i + e)], preferred_element_type=F32)
            land("sib", k, s, i)
            c = p + pr[k, s, i]
            cb = c.astype(BF16)
            cc[k, s, i] = c
            cs[k, s, i] = cb
            if k == 0:
                cl[s, i] = (c - cb.astype(F32)).astype(BF16)
            launch(("x", k, s, i), x_copy(k, s, i))

    def gather(k, s, i):
        land("x", k, s, i)
        v = cc[k, s, i] + cr[k, s, i].astype(F32)
        cc[k, s, i] = v
        vop[k, s, 2 * i + e] = v.astype(BF16)
        launch(("ag", k, s, i), ag_copy(k, s, i, 2 * i + e))

    def transpose_operator():
        at = [lax.broadcasted_iota(jnp.int32, (256, 256), d) for d in range(2)]
        eye[...] = jnp.where(at[0] == at[1], 1.0, 0.0).astype(BF16)

        def go(b, c):
            for q in range(2):
                for part in range(2):
                    for n in range(2):
                        rows = slice(part * ROWS + n * 512, part * ROWS + (n + 1) * 512)
                        col = pl.multiple_of(b * BLK + q * 256, 256)
                        ot[b, part * BLK + q * 256 : part * BLK + (q + 1) * 256, n * 512 : (n + 1) * 512] = nt_dot(
                            eye[...], op[rows, pl.ds(col, 256)]
                        ).astype(BF16)
            return c

        lax.fori_loop(0, 4, go, 0)

    def forward_block(k, s, b, dst, first):
        v = vop[k, s, b]
        xc[:, 0:BLK] = v
        xc[0:64, BLK:] = -v[64:128]
        xc[64:128, BLK:] = v[0:64]
        for n in range(2):
            lo, hi = n * 512, (n + 1) * 512
            part = jnp.dot(xc[...], ot[b, :, lo:hi], preferred_element_type=F32)
            if first:
                dst[s, :, lo:hi] = part
            else:
                dst[s, :, lo:hi] += part

    def forward(k, s, i, dst):
        forward_block(k, s, 2 * i + e, dst, i == 0)
        land("ag", k, s, i)
        forward_block(k, s, 2 * i + 1 - e, dst, False)

    def operand(s):
        y = (yy[s] * TAU).astype(BF16)
        xy[s, :, 0:ROWS] = y
        xy[s, 0:64, ROWS:] = y[64:128]
        xy[s, 64:128, ROWS:] = -y[0:64]

    def ar_start(n, tile):
        ar_src[n] = tile
        ar1[n, 0] = tile

        for d in AR_NEAR:
            remote(ar_src.at[n], ar1.at[n, d], r_ss.at[n, 0], r_rs.at[n, 0], peer1(d)).start()
        ar_flying(n, 0, ar1)

    def ar_flying(n, stage, ref):
        part = ref.at[n, pl.ds(1, 15)]
        flying[("ar", n, stage), "send"] = local(part, part, r_ss.at[n, stage]).wait
        flying[("ar", n, stage), "recv"] = local(part, part, r_rs.at[n, stage]).wait

    def ar_middle(n):
        land("ar", n, 0)
        tile = jnp.sum(ar1[n], axis=0)
        ar_mid[n] = tile
        ar2[n, 0] = tile

        for d in AR_FAR:
            remote(ar_mid.at[n], ar2.at[n, d], r_ss.at[n, 1], r_rs.at[n, 1], peer2(d)).start()
        ar_flying(n, 1, ar2)

    def ar_end(n):
        land("ar", n, 1)
        return jnp.sum(jnp.sum(ar2[n], axis=0), axis=1, keepdims=True)

    def tile_of(rows):
        at = lax.broadcasted_iota(jnp.int32, (8, 128), 0)
        tile = jnp.zeros((8, 128), F32)
        for i, row in enumerate(rows):
            tile = jnp.where(at == i, row, tile)
        return tile

    def body():
        land("tb")
        dft(0)
        pl.semaphore_wait(barrier, FREQS - 1 + 12)
        a2a_send(0)
        dft(1)
        land("op")
        transpose_operator()
        a2a_send(1)

        zero = jnp.zeros((1, 128), F32)
        sum_u = zero
        for s in range(2):
            land("a2a", s)
            sum_u = sum_u + relayout(s)
            adjoint(0, xu, s)

        sum_v, sum_y, sum_yu = zero, zero, zero
        for s in range(2):
            for i in range(2):
                gather(0, s, i)
                forward(0, s, i, yy)
            operand(s)
            adjoint(1, xy, s)
            v = cc[0, s, h]
            sum_v = sum_v + lane_sums(v * v)
            sum_y = sum_y + lane_sums(yy[s] * yy[s])
            sum_yu = sum_yu + lane_sums(yy[s] * xu[s, :, 0:ROWS].astype(F32))
            if s == 0:
                ar_start(0, tile_of([sum_u, sum_v, sum_y]))
        ar_middle(0)

        sum_r, sum_rv, sum_g, sum_gy, sum_gu = zero, zero, zero, zero, zero
        for i in range(2):
            gather(1, 0, i)
            forward(1, 0, i, zz)
        gather(1, 1, 0)
        forward(1, 1, 0, zz)
        total = ar_end(0)
        s_u = total[0:1]
        kappa = total[2:3] / jnp.maximum(total[1:2], 1e-30) * TAU
        for s in range(2):
            if s == 1:
                gather(1, 1, 1)
                for t in range(2):
                    launch(("lo", t), lo_copy(t))
                forward(1, 1, 1, zz)
            v = cc[0, s, h]
            right = cc[1, s, h] - kappa * v
            sum_r = sum_r + lane_sums(right * right)
            sum_rv = sum_rv + lane_sums(right * v)
            y = yy[s]
            ahead = zz[s] - kappa * y
            sum_g = sum_g + lane_sums(ahead * ahead)
            sum_gy = sum_gy + lane_sums(ahead * y)
            sum_gu = sum_gu + lane_sums(ahead * xu[s, :, 0:ROWS].astype(F32))
        ar_start(1, tile_of([sum_v, sum_y, sum_yu, sum_r, sum_rv, sum_g, sum_gy, sum_gu]))
        for s in range(2):
            land("lo", s)
        ar_middle(1)
        total = ar_end(1)
        s_v, s_y, s_yu, s_r, s_rv, s_g, s_gy, s_gu = (total[i : i + 1] for i in range(8))
        beta0 = jnp.sqrt(s_u * (1.0 / SIGMA**2) + EPS)
        sb0 = beta0 * SIGMA
        alpha0_sq = s_v / (sb0 * sb0) + EPS
        alpha0 = jnp.sqrt(alpha0_sq)
        g0 = sb0 * alpha0
        s_left = jnp.maximum(s_y - alpha0_sq * (2.0 * s_yu - alpha0_sq * s_u), 0.0)
        beta1_sq = s_left / (g0 * g0) + EPS
        beta1 = jnp.sqrt(beta1_sq)
        k1 = (alpha0_sq + beta1_sq) * TAU
        delta = k1 - kappa
        s_r = jnp.maximum(s_r - delta * (2.0 * s_rv - delta * s_v), 0.0)
        s_gl = s_gy - alpha0_sq * s_gu - delta * (s_y - alpha0_sq * s_yu)
        s_g = jnp.maximum(s_g - delta * (2.0 * s_gy - delta * s_y), 0.0)
        g1s = g0 * beta1 * TAU
        alpha1_sq = s_r / (g1s * g1s) + EPS
        alpha1 = jnp.sqrt(alpha1_sq)
        g2s = g1s * alpha1
        a_sq = alpha1_sq * TAU
        s_left2 = jnp.maximum(s_g - a_sq * (2.0 * s_gl - a_sq * s_left), 0.0)
        beta2_sq = s_left2 / (g2s * g2s) + EPS

        rho1_sq = alpha0_sq + beta1_sq
        rho1 = jnp.sqrt(rho1_sq)
        cos1 = alpha0 / rho1
        sin1 = beta1 / rho1
        theta1 = sin1 * alpha1
        rhobar = cos1 * alpha1
        phi1 = cos1 * beta0
        phibar = sin1 * beta0
        rho2 = jnp.sqrt(rhobar * rhobar + beta2_sq)
        phi2 = (rhobar / rho2) * phibar
        y2 = -(phi2 / rho2)
        c_v = (phi1 / rho1 - y2 * (theta1 / rho1)) / g0
        c_r = y2 / g2s
        for s in range(2):
            v = cc[0, s, h] + clr[s].astype(F32)
            right = cc[1, s, h] - k1 * v
            x = c_v * v + c_r * right
            for c in range(2):
                for t in range(4):
                    tmp[t, pl.ds(c * 128 + s, 64, stride=2), :] = x[
                        c * 64 : (c + 1) * 64, t * 128 : (t + 1) * 128
                    ]
        for c in range(2):
            for t in range(4):
                out_ref[pl.ds(t * 256 + c, 128, stride=2), :] = tmp[t, c * 128 : (c + 1) * 128, :].T

    body()
    for wait in flying.values():
        wait()


def per_device(table, traces, downgoing):
    vmem = pltpu.VMEM
    dma = pltpu.SemaphoreType.DMA
    scratch = [
        vmem((4 * FREQS, SAMPLES), BF16),
        vmem((2, ROWS, SAMPLES), BF16),
        vmem((2 * ROWS, COLS), BF16),
        vmem((FREQS * 16, 128), F32),
        vmem((FREQS * 16, 128), F32),
        vmem((FREQS, 32, 128), BF16),
        vmem((FREQS, 32, 128), BF16),
        vmem((2, M, 2 * ROWS), BF16),
        vmem((2, M, 2 * ROWS), BF16),
        vmem((2, 2, 2, M, BLK), F32),
        vmem((2, 2, 2, M, BLK), F32),
        vmem((2, 2, 2, M, BLK), F32),
        vmem((2, 2, 2, M, BLK), BF16),
        vmem((2, 2, 2, M, BLK), BF16),
        vmem((2, 2, M, BLK), BF16),
        vmem((2, M, BLK), BF16),
        vmem((2, 2, 4, M, BLK), BF16),
        vmem((M, 2 * BLK), BF16),
        vmem((256, 256), BF16),
        vmem((4, 2 * BLK, ROWS), BF16),
        vmem((2, M, ROWS), F32),
        vmem((2, M, ROWS), F32),
        vmem((4, 2 * M, 128), F32),
        vmem((2, 8, 128), F32),
        vmem((2, 16, 8, 128), F32),
        vmem((2, 8, 128), F32),
        vmem((2, 16, 8, 128), F32),
        dma, dma((2,)), dma,
        dma((2,)), dma((2,)),
        dma((2, 2, 2)), dma((2, 2, 2)),
        dma((2, 2, 2)), dma((2, 2, 2)),
        dma((2, 2, 2)), dma((2, 2, 2)),
        dma((2,)), dma((2,)),
        dma((2, 2)), dma((2, 2)),
    ]
    out = pl.pallas_call(
        kernel,
        out_shape=jax.ShapeDtypeStruct((2 * BLK, 128), F32),
        in_specs=[
            pl.BlockSpec(memory_space=pl.ANY),
            pl.BlockSpec(memory_space=pl.ANY),
            pl.BlockSpec(memory_space=pl.ANY),
        ],
        out_specs=pl.BlockSpec(memory_space=pltpu.VMEM),
        scratch_shapes=scratch,
        compiler_params=pltpu.CompilerParams(
            collective_id=0, has_side_effects=True, vmem_limit_bytes=63 * 2**20
        ),
        name="lsqr",
    )(table, traces, downgoing.reshape(2 * ROWS, COLS))
    return out.reshape(1, BLK, 2, 128)


def solution(mesh):
    table = dft_table()
    return jax.shard_map(
        lambda traces, downgoing: per_device(jnp.asarray(table), traces, downgoing),
        mesh=mesh,
        in_specs=(P("freq", "rcv", None), P("freq", None, "rcv", None)),
        out_specs=P("freq", "rcv", None, None),
        check_vma=False,
    )
```

```python
import math

import jax
import jax.numpy as jnp
import ml_dtypes
import numpy as np
from jax import lax
from jax.experimental import pallas as pl
from jax.experimental.pallas import tpu as pltpu
from jax.sharding import PartitionSpec as P

EPS = 1e-06
MESH = pl.DeviceIdType.MESH
BF16 = jnp.bfloat16
F32 = jnp.float32
FREQS = 64
RCV = 4
SAMPLES = 1024
ROWS = 1024
COLS = 2048
BLK = 512
M = 128
SIGMA = 2.0**-10
FAR_FIRST = (4, 3, 5, 2, 6, 1, 7, 0)
AR_NEAR = (8, 9, 7, 6, 10, 5, 11, 4, 12, 3, 13, 2, 14, 1, 15)
AR_FAR = (10, 9, 11, 8, 6, 14, 5, 7, 13, 15, 2, 4, 12, 1, 3)
TAU = 2.0**-8


def dft_table():
    times = np.arange(SAMPLES, dtype=np.int64)
    bins = np.arange(FREQS, dtype=np.int64) + 1
    phase = (bins[:, None] * times[None, :] % SAMPLES).astype(np.float64) * (2.0 * math.pi / SAMPLES)
    table = np.concatenate([np.cos(phase), -np.sin(phase)], axis=0) * SIGMA
    high = table.astype(ml_dtypes.bfloat16)
    low = (table - high.astype(np.float64)).astype(ml_dtypes.bfloat16)
    return np.concatenate([high, low], axis=0)


def lane_sums(x):
    acc = x[:, 0:128]
    for t in range(1, x.shape[1] // 128):
        acc = acc + x[:, t * 128 : (t + 1) * 128]
    return jnp.sum(acc, axis=0, keepdims=True)


def nt_dot(a, b):
    return lax.dot_general(a, b, (((1,), (1,)), ((), ())), preferred_element_type=F32)


def kernel(
    table_ref, traces_ref, oper_ref, out_ref,
    tb, tr, op, s32, f32s, sb, rb, xu, xy, ps, pr, cc, cs, cr, cl, clr, vop, xc, eye, ot, yy, zz, tmp,
    ar_src, ar1, ar_mid, ar2,
    tb_sem, tr_sem, op_sem, a_ss, a_rs, p_ss, p_rs, x_ss, x_rs, g_ss, g_rs, l_ss, l_rs, r_ss, r_rs,
):
    f = lax.axis_index("freq")
    r = lax.axis_index("rcv")
    h = r // 2
    e = lax.rem(r, 2)
    sib = (f, h * 2 + 1 - e)
    xp = (f, (1 - h) * 2 + e)
    g1 = lax.rem(f, 16)
    fy = f // 16
    fz = g1 // 2
    fl = lax.rem(f, 2)

    def peer1(d):
        return (fy * 16 + lax.rem(g1 + d, 16), r)

    def peer2(d):
        return (lax.rem(fy + d // 4, 4) * 16 + g1, lax.rem(r + lax.rem(d, 4), 4))

    def local(src, dst, sem):
        return pltpu.make_async_copy(src, dst, sem)

    def remote(src, dst, ss, rs, to):
        return pltpu.make_async_remote_copy(
            src_ref=src, dst_ref=dst, send_sem=ss, recv_sem=rs, device_id=to, device_id_type=MESH
        )

    flying = {}

    def launch(key, copy):
        copy.start()
        flying[key, "send"] = copy.wait_send
        flying[key, "recv"] = copy.wait_recv

    def land(*key):
        flying.pop((key, "recv"))()

    tb_copy = local(table_ref, tb, tb_sem)
    tb_copy.start()
    flying[("tb",), "recv"] = tb_copy.wait
    tr_copies = [local(traces_ref.at[s], tr.at[s], tr_sem.at[s]) for s in range(2)]
    for s in range(2):
        tr_copies[s].start()
        flying[("tr", s), "recv"] = tr_copies[s].wait

    barrier = pltpu.get_barrier_semaphore()

    def each_freq_peer(act):
        for dz in FAR_FIRST:

            def go(q, c, dz=dz):
                y = lax.rem(fy + q // 2, 4)
                z = lax.rem(fz + dz, 8)
                lo = lax.rem(fl + lax.rem(q, 2), 2)
                act(y * 16 + z * 2 + lo)
                return c

            lax.fori_loop(1 if dz == 0 else 0, 8, go, 0)

    def greet2(d, c):
        to = (lax.rem(fy + d // 3, 4) * 16 + g1, lax.rem(r + 1 + lax.rem(d, 3), 4))
        pl.semaphore_signal(barrier, inc=1, device_id=to, device_id_type=MESH)
        return c

    def greet(to):
        pl.semaphore_signal(barrier, inc=1, device_id=(to, r), device_id_type=MESH)

    lax.fori_loop(0, 12, greet2, 0)
    each_freq_peer(greet)

    op_copy = local(oper_ref, op, op_sem)
    op_copy.start()
    flying[("op",), "recv"] = op_copy.wait

    def dft(s):
        land("tr", s)
        for q in range(4):
            res = nt_dot(tb[...], tr[s, q * 256 : (q + 1) * 256, :])
            d = res[0:128] + res[128:256]
            for c in range(2):
                for qq in range(2):
                    s32[pl.ds((q * 2 + qq) * 2 + c, FREQS, stride=16), :] = d[
                        c * 64 : (c + 1) * 64, qq * 128 : (qq + 1) * 128
                    ]
        sb[:, s * 16 : (s + 1) * 16, :] = s32[...].astype(BF16).reshape(FREQS, 16, 128)

    def a2a_send(s):
        def go(to):
            part = pl.ds(s * 16, 16)
            remote(sb.at[to, part], rb.at[f, part], a_ss.at[s], a_rs.at[s], (to, r)).start()

        each_freq_peer(go)
        rb[f, s * 16 : (s + 1) * 16] = sb[f, s * 16 : (s + 1) * 16]
        most = (pl.ds(0, FREQS - 1), pl.ds(s * 16, 16))
        sent, got = sb.at[most], rb.at[most]
        flying[("a2a", s), "send"] = local(sent, sent, a_ss.at[s]).wait
        flying[("a2a", s), "recv"] = local(got, got, a_rs.at[s]).wait

    def relayout(s):
        f32s[...] = rb[:, s * 16 : (s + 1) * 16, :].astype(F32).reshape(FREQS * 16, 128)
        total = jnp.zeros((FREQS, 128), F32)
        for q in range(8):
            lo, hi = q * 128, (q + 1) * 128
            re = f32s[pl.ds(q * 2, FREQS, stride=16), :]
            im = f32s[pl.ds(q * 2 + 1, FREQS, stride=16), :]
            total = total + re * re + im * im
            reb, imb = re.astype(BF16), im.astype(BF16)
            xu[s, 0:64, lo:hi] = reb
            xu[s, 64:128, lo:hi] = imb
            xu[s, 0:64, ROWS + lo : ROWS + hi] = imb
            xu[s, 64:128, ROWS + lo : ROWS + hi] = -reb
        return jnp.sum(total, axis=0, keepdims=True)

    def cols(b):
        return pl.ds(pl.multiple_of(b * BLK, BLK), BLK)

    def sib_copy(k, s, i):
        return remote(ps.at[k, s, i], pr.at[k, s, i], p_ss.at[k, s, i], p_rs.at[k, s, i], sib)

    def x_copy(k, s, i):
        return remote(cs.at[k, s, i], cr.at[k, s, i], x_ss.at[k, s, i], x_rs.at[k, s, i], xp)

    def ag_copy(k, s, i, b):
        part = vop.at[k, s, b]
        return remote(part, part, g_ss.at[k, s, i], g_rs.at[k, s, i], sib)

    def lo_copy(s):
        return remote(cl.at[s, 1 - h], clr.at[s], l_ss.at[s], l_rs.at[s], xp)

    def adjoint(k, x, s):
        def part(b):
            return jnp.dot(x[s], op[:, cols(b)], preferred_element_type=F32)

        ps[k, s, 0] = part(1 - e)
        launch(("sib", k, s, 0), sib_copy(k, s, 0))
        cc[k, s, 0] = part(e)
        ps[k, s, 1] = part(2 + 1 - e)
        launch(("sib", k, s, 1), sib_copy(k, s, 1))
        for i in range(2):
            if i == 1:
                cc[k, s, 1] = part(2 + e)
            land("sib", k, s, i)
            c = cc[k, s, i] + pr[k, s, i]
            cb = c.astype(BF16)
            cc[k, s, i] = c
            cs[k, s, i] = cb
            if k == 0:
                cl[s, i] = (c - cb.astype(F32)).astype(BF16)
            launch(("x", k, s, i), x_copy(k, s, i))

    def gather(k, s, i):
        land("x", k, s, i)
        v = cc[k, s, i] + cr[k, s, i].astype(F32)
        cc[k, s, i] = v
        vop[k, s, 2 * i + e] = v.astype(BF16)
        launch(("ag", k, s, i), ag_copy(k, s, i, 2 * i + e))

    def transpose_operator():
        at = [lax.broadcasted_iota(jnp.int32, (256, 256), d) for d in range(2)]
        eye[...] = jnp.where(at[0] == at[1], 1.0, 0.0).astype(BF16)

        def go(b, c):
            for q in range(2):
                for part in range(2):
                    for n in range(2):
                        rows = slice(part * ROWS + n * 512, part * ROWS + (n + 1) * 512)
                        col = pl.multiple_of(b * BLK + q * 256, 256)
                        ot[b, part * BLK + q * 256 : part * BLK + (q + 1) * 256, n * 512 : (n + 1) * 512] = nt_dot(
                            eye[...], op[rows, pl.ds(col, 256)]
                        ).astype(BF16)
            return c

        lax.fori_loop(0, 4, go, 0)

    def forward_block(k, s, b, dst, first):
        v = vop[k, s, b]
        xc[:, 0:BLK] = v
        xc[0:64, BLK:] = -v[64:128]
        xc[64:128, BLK:] = v[0:64]
        for n in range(2):
            lo, hi = n * 512, (n + 1) * 512
            part = jnp.dot(xc[...], ot[b, :, lo:hi], preferred_element_type=F32)
            if first:
                dst[s, :, lo:hi] = part
            else:
                dst[s, :, lo:hi] += part

    def forward(k, s, i, dst):
        forward_block(k, s, 2 * i + e, dst, i == 0)
        land("ag", k, s, i)
        forward_block(k, s, 2 * i + 1 - e, dst, False)

    def operand(s):
        y = (yy[s] * TAU).astype(BF16)
        xy[s, :, 0:ROWS] = y
        xy[s, 0:64, ROWS:] = y[64:128]
        xy[s, 64:128, ROWS:] = -y[0:64]

    def ar_start(n, tile):
        ar_src[n] = tile
        ar1[n, 0] = tile

        for d in AR_NEAR:
            remote(ar_src.at[n], ar1.at[n, d], r_ss.at[n, 0], r_rs.at[n, 0], peer1(d)).start()
        ar_flying(n, 0, ar1)

    def ar_flying(n, stage, ref):
        part = ref.at[n, pl.ds(1, 15)]
        flying[("ar", n, stage), "send"] = local(part, part, r_ss.at[n, stage]).wait
        flying[("ar", n, stage), "recv"] = local(part, part, r_rs.at[n, stage]).wait

    def ar_middle(n):
        land("ar", n, 0)
        tile = jnp.sum(ar1[n], axis=0)
        ar_mid[n] = tile
        ar2[n, 0] = tile

        for d in AR_FAR:
            remote(ar_mid.at[n], ar2.at[n, d], r_ss.at[n, 1], r_rs.at[n, 1], peer2(d)).start()
        ar_flying(n, 1, ar2)

    def ar_end(n):
        land("ar", n, 1)
        return jnp.sum(jnp.sum(ar2[n], axis=0), axis=1, keepdims=True)

    def tile_of(rows):
        at = lax.broadcasted_iota(jnp.int32, (8, 128), 0)
        tile = jnp.zeros((8, 128), F32)
        for i, row in enumerate(rows):
            tile = jnp.where(at == i, row, tile)
        return tile

    def body():
        land("tb")
        dft(0)
        pl.semaphore_wait(barrier, FREQS - 1 + 12)
        a2a_send(0)
        dft(1)
        land("op")
        transpose_operator()
        a2a_send(1)

        zero = jnp.zeros((1, 128), F32)
        sum_u = zero
        for s in range(2):
            land("a2a", s)
            sum_u = sum_u + relayout(s)
            adjoint(0, xu, s)

        sum_v, sum_y, sum_yu = zero, zero, zero
        for s in range(2):
            for i in range(2):
                gather(0, s, i)
                forward(0, s, i, yy)
            operand(s)
            adjoint(1, xy, s)
            v = cc[0, s, h]
            sum_v = sum_v + lane_sums(v * v)
            sum_y = sum_y + lane_sums(yy[s] * yy[s])
            sum_yu = sum_yu + lane_sums(yy[s] * xu[s, :, 0:ROWS].astype(F32))
            if s == 0:
                ar_start(0, tile_of([sum_u, sum_v, sum_y]))
        ar_middle(0)

        sum_r, sum_rv, sum_g, sum_gy, sum_gu = zero, zero, zero, zero, zero
        for i in range(2):
            gather(1, 0, i)
            forward(1, 0, i, zz)
        gather(1, 1, 0)
        forward(1, 1, 0, zz)
        total = ar_end(0)
        s_u = total[0:1]
        kappa = total[2:3] / jnp.maximum(total[1:2], 1e-30) * TAU
        for s in range(2):
            zz[s] -= kappa * yy[s]
            if s == 1:
                gather(1, 1, 1)
                for t in range(2):
                    launch(("lo", t), lo_copy(t))
            v = cc[0, s, h]
            right = cc[1, s, h] - kappa * v
            sum_r = sum_r + lane_sums(right * right)
            sum_rv = sum_rv + lane_sums(right * v)
            if s == 1:
                forward(1, 1, 1, zz)
            y = yy[s]
            ahead = zz[s]
            sum_g = sum_g + lane_sums(ahead * ahead)
            sum_gy = sum_gy + lane_sums(ahead * y)
            sum_gu = sum_gu + lane_sums(ahead * xu[s, :, 0:ROWS].astype(F32))
        ar_start(1, tile_of([sum_v, sum_y, sum_yu, sum_r, sum_rv, sum_g, sum_gy, sum_gu]))
        ar_middle(1)
        total = ar_end(1)
        s_v, s_y, s_yu, s_r, s_rv, s_g, s_gy, s_gu = (total[i : i + 1] for i in range(8))
        beta0 = jnp.sqrt(s_u * (1.0 / SIGMA**2) + EPS)
        sb0 = beta0 * SIGMA
        alpha0_sq = s_v / (sb0 * sb0) + EPS
        alpha0 = jnp.sqrt(alpha0_sq)
        g0 = sb0 * alpha0
        s_left = jnp.maximum(s_y - alpha0_sq * (2.0 * s_yu - alpha0_sq * s_u), 0.0)
        beta1_sq = s_left / (g0 * g0) + EPS
        beta1 = jnp.sqrt(beta1_sq)
        k1 = (alpha0_sq + beta1_sq) * TAU
        delta = k1 - kappa
        s_r = jnp.maximum(s_r - delta * (2.0 * s_rv - delta * s_v), 0.0)
        s_gl = s_gy - alpha0_sq * s_gu - delta * (s_y - alpha0_sq * s_yu)
        s_g = jnp.maximum(s_g - delta * (2.0 * s_gy - delta * s_y), 0.0)
        g1s = g0 * beta1 * TAU
        alpha1_sq = s_r / (g1s * g1s) + EPS
        alpha1 = jnp.sqrt(alpha1_sq)
        g2s = g1s * alpha1
        a_sq = alpha1_sq * TAU
        s_left2 = jnp.maximum(s_g - a_sq * (2.0 * s_gl - a_sq * s_left), 0.0)
        beta2_sq = s_left2 / (g2s * g2s) + EPS

        rho1_sq = alpha0_sq + beta1_sq
        rho1 = jnp.sqrt(rho1_sq)
        cos1 = alpha0 / rho1
        sin1 = beta1 / rho1
        theta1 = sin1 * alpha1
        rhobar = cos1 * alpha1
        phi1 = cos1 * beta0
        phibar = sin1 * beta0
        rho2 = jnp.sqrt(rhobar * rhobar + beta2_sq)
        phi2 = (rhobar / rho2) * phibar
        y2 = -(phi2 / rho2)
        c_v = (phi1 / rho1 - y2 * (theta1 / rho1)) / g0
        c_r = y2 / g2s
        for s in range(2):
            land("lo", s)
            v = cc[0, s, h] + clr[s].astype(F32)
            right = cc[1, s, h] - k1 * v
            x = c_v * v + c_r * right
            for c in range(2):
                for t in range(4):
                    tmp[t, pl.ds(c * 128 + s, 64, stride=2), :] = x[
                        c * 64 : (c + 1) * 64, t * 128 : (t + 1) * 128
                    ]
        for c in range(2):
            for t in range(4):
                out_ref[pl.ds(t * 256 + c, 128, stride=2), :] = tmp[t, c * 128 : (c + 1) * 128, :].T

    body()
    for wait in flying.values():
        wait()


def per_device(table, traces, downgoing):
    vmem = pltpu.VMEM
    dma = pltpu.SemaphoreType.DMA
    scratch = [
        vmem((4 * FREQS, SAMPLES), BF16),
        vmem((2, ROWS, SAMPLES), BF16),
        vmem((2 * ROWS, COLS), BF16),
        vmem((FREQS * 16, 128), F32),
        vmem((FREQS * 16, 128), F32),
        vmem((FREQS, 32, 128), BF16),
        vmem((FREQS, 32, 128), BF16),
        vmem((2, M, 2 * ROWS), BF16),
        vmem((2, M, 2 * ROWS), BF16),
        vmem((2, 2, 2, M, BLK), F32),
        vmem((2, 2, 2, M, BLK), F32),
        vmem((2, 2, 2, M, BLK), F32),
        vmem((2, 2, 2, M, BLK), BF16),
        vmem((2, 2, 2, M, BLK), BF16),
        vmem((2, 2, M, BLK), BF16),
        vmem((2, M, BLK), BF16),
        vmem((2, 2, 4, M, BLK), BF16),
        vmem((M, 2 * BLK), BF16),
        vmem((256, 256), BF16),
        vmem((4, 2 * BLK, ROWS), BF16),
        vmem((2, M, ROWS), F32),
        vmem((2, M, ROWS), F32),
        vmem((4, 2 * M, 128), F32),
        vmem((2, 8, 128), F32),
        vmem((2, 16, 8, 128), F32),
        vmem((2, 8, 128), F32),
        vmem((2, 16, 8, 128), F32),
        dma, dma((2,)), dma,
        dma((2,)), dma((2,)),
        dma((2, 2, 2)), dma((2, 2, 2)),
        dma((2, 2, 2)), dma((2, 2, 2)),
        dma((2, 2, 2)), dma((2, 2, 2)),
        dma((2,)), dma((2,)),
        dma((2, 2)), dma((2, 2)),
    ]
    out = pl.pallas_call(
        kernel,
        out_shape=jax.ShapeDtypeStruct((2 * BLK, 128), F32),
        in_specs=[
            pl.BlockSpec(memory_space=pl.ANY),
            pl.BlockSpec(memory_space=pl.ANY),
            pl.BlockSpec(memory_space=pl.ANY),
        ],
        out_specs=pl.BlockSpec(memory_space=pltpu.VMEM),
        scratch_shapes=scratch,
        compiler_params=pltpu.CompilerParams(
            collective_id=0, has_side_effects=True, vmem_limit_bytes=63 * 2**20
        ),
        name="lsqr",
    )(table, traces, downgoing.reshape(2 * ROWS, COLS))
    return out.reshape(1, BLK, 2, 128)


def solution(mesh):
    table = dft_table()
    return jax.shard_map(
        lambda traces, downgoing: per_device(jnp.asarray(table), traces, downgoing),
        mesh=mesh,
        in_specs=(P("freq", "rcv", None), P("freq", None, "rcv", None)),
        out_specs=P("freq", "rcv", None, None),
        check_vma=False,
    )
```

```python
import math

import jax
import jax.numpy as jnp
import ml_dtypes
import numpy as np
from jax import lax
from jax.experimental import pallas as pl
from jax.experimental.pallas import tpu as pltpu
from jax.sharding import PartitionSpec as P

EPS = 1e-06
MESH = pl.DeviceIdType.MESH
BF16 = jnp.bfloat16
F32 = jnp.float32
FREQS = 64
RCV = 4
SAMPLES = 1024
ROWS = 1024
COLS = 2048
BLK = 512
M = 128
SIGMA = 2.0**-10
FAR_FIRST = (4, 3, 5, 2, 6, 1, 7, 0)
AR_NEAR = (8, 9, 7, 6, 10, 5, 11, 4, 12, 3, 13, 2, 14, 1, 15)
AR_FAR = (10, 9, 11, 8, 6, 14, 5, 7, 13, 15, 2, 4, 12, 1, 3)
TAU = 2.0**-8


def dft_table():
    times = np.arange(SAMPLES, dtype=np.int64)
    bins = np.arange(FREQS, dtype=np.int64) + 1
    phase = (bins[:, None] * times[None, :] % SAMPLES).astype(np.float64) * (2.0 * math.pi / SAMPLES)
    table = np.concatenate([np.cos(phase), -np.sin(phase)], axis=0) * SIGMA
    high = table.astype(ml_dtypes.bfloat16)
    low = (table - high.astype(np.float64)).astype(ml_dtypes.bfloat16)
    return np.concatenate([high, low], axis=0)


def lane_sums(x):
    acc = x[:, 0:128]
    for t in range(1, x.shape[1] // 128):
        acc = acc + x[:, t * 128 : (t + 1) * 128]
    return jnp.sum(acc, axis=0, keepdims=True)


def nt_dot(a, b):
    return lax.dot_general(a, b, (((1,), (1,)), ((), ())), preferred_element_type=F32)


def kernel(
    table_ref, traces_ref, oper_ref, out_ref,
    tb, tr, op, s32, f32s, sb, rb, xu, xy, ps, pr, cc, cs, cr, cl, clr, vop, xc, eye, ot, yy, zz, tmp,
    ar_src, ar1, ar_mid, ar2,
    tb_sem, tr_sem, op_sem, a_ss, a_rs, p_ss, p_rs, x_ss, x_rs, g_ss, g_rs, l_ss, l_rs, r_ss, r_rs,
):
    f = lax.axis_index("freq")
    r = lax.axis_index("rcv")
    h = r // 2
    e = lax.rem(r, 2)
    sib = (f, h * 2 + 1 - e)
    xp = (f, (1 - h) * 2 + e)
    g1 = lax.rem(f, 16)
    fy = f // 16
    fz = g1 // 2
    fl = lax.rem(f, 2)

    def peer1(d):
        return (fy * 16 + lax.rem(g1 + d, 16), r)

    def peer2(d):
        return (lax.rem(fy + d // 4, 4) * 16 + g1, lax.rem(r + lax.rem(d, 4), 4))

    def local(src, dst, sem):
        return pltpu.make_async_copy(src, dst, sem)

    def remote(src, dst, ss, rs, to):
        return pltpu.make_async_remote_copy(
            src_ref=src, dst_ref=dst, send_sem=ss, recv_sem=rs, device_id=to, device_id_type=MESH
        )

    flying = {}

    def launch(key, copy):
        copy.start()
        flying[key, "send"] = copy.wait_send
        flying[key, "recv"] = copy.wait_recv

    def land(*key):
        flying.pop((key, "recv"))()

    tb_copy = local(table_ref, tb, tb_sem)
    tb_copy.start()
    flying[("tb",), "recv"] = tb_copy.wait
    tr_copies = [local(traces_ref.at[s], tr.at[s], tr_sem.at[s]) for s in range(2)]
    for s in range(2):
        tr_copies[s].start()
        flying[("tr", s), "recv"] = tr_copies[s].wait

    barrier = pltpu.get_barrier_semaphore()

    def each_freq_peer(act):
        for dz in FAR_FIRST:

            def go(q, c, dz=dz):
                y = lax.rem(fy + 2 + q // 2, 4)
                z = lax.rem(fz + dz, 8)
                lo = lax.rem(fl + 1 + lax.rem(q, 2), 2)
                act(y * 16 + z * 2 + lo)
                return c

            if dz == 0:
                lax.fori_loop(0, 5, go, 0)
                lax.fori_loop(6, 8, go, 0)
            else:
                lax.fori_loop(0, 8, go, 0)

    def greet2(d, c):
        to = (lax.rem(fy + d // 3, 4) * 16 + g1, lax.rem(r + 1 + lax.rem(d, 3), 4))
        pl.semaphore_signal(barrier, inc=1, device_id=to, device_id_type=MESH)
        return c

    def greet(to):
        pl.semaphore_signal(barrier, inc=1, device_id=(to, r), device_id_type=MESH)

    lax.fori_loop(0, 12, greet2, 0)
    each_freq_peer(greet)

    op_copy = local(oper_ref, op, op_sem)
    op_copy.start()
    flying[("op",), "recv"] = op_copy.wait

    def dft(s):
        land("tr", s)
        for q in range(4):
            res = nt_dot(tb[...], tr[s, q * 256 : (q + 1) * 256, :])
            d = res[0:128] + res[128:256]
            for c in range(2):
                for qq in range(2):
                    s32[pl.ds((q * 2 + qq) * 2 + c, FREQS, stride=16), :] = d[
                        c * 64 : (c + 1) * 64, qq * 128 : (qq + 1) * 128
                    ]
        sb[:, s * 16 : (s + 1) * 16, :] = s32[...].astype(BF16).reshape(FREQS, 16, 128)

    def a2a_send(s):
        def go(to):
            part = pl.ds(s * 16, 16)
            remote(sb.at[to, part], rb.at[f, part], a_ss.at[s], a_rs.at[s], (to, r)).start()

        each_freq_peer(go)
        rb[f, s * 16 : (s + 1) * 16] = sb[f, s * 16 : (s + 1) * 16]
        most = (pl.ds(0, FREQS - 1), pl.ds(s * 16, 16))
        sent, got = sb.at[most], rb.at[most]
        flying[("a2a", s), "send"] = local(sent, sent, a_ss.at[s]).wait
        flying[("a2a", s), "recv"] = local(got, got, a_rs.at[s]).wait

    def relayout(s):
        f32s[...] = rb[:, s * 16 : (s + 1) * 16, :].astype(F32).reshape(FREQS * 16, 128)
        total = jnp.zeros((FREQS, 128), F32)
        for q in range(8):
            lo, hi = q * 128, (q + 1) * 128
            re = f32s[pl.ds(q * 2, FREQS, stride=16), :]
            im = f32s[pl.ds(q * 2 + 1, FREQS, stride=16), :]
            total = total + re * re + im * im
            reb, imb = re.astype(BF16), im.astype(BF16)
            xu[s, 0:64, lo:hi] = reb
            xu[s, 64:128, lo:hi] = imb
            xu[s, 0:64, ROWS + lo : ROWS + hi] = imb
            xu[s, 64:128, ROWS + lo : ROWS + hi] = -reb
        return jnp.sum(total, axis=0, keepdims=True)

    def cols(b):
        return pl.ds(pl.multiple_of(b * BLK, BLK), BLK)

    def sib_copy(k, s, i):
        return remote(ps.at[k, s, i], pr.at[k, s, i], p_ss.at[k, s, i], p_rs.at[k, s, i], sib)

    def x_copy(k, s, i):
        return remote(cs.at[k, s, i], cr.at[k, s, i], x_ss.at[k, s, i], x_rs.at[k, s, i], xp)

    def ag_copy(k, s, i, b):
        part = vop.at[k, s, b]
        return remote(part, part, g_ss.at[k, s, i], g_rs.at[k, s, i], sib)

    def lo_copy(s):
        return remote(cl.at[s, 1 - h], clr.at[s], l_ss.at[s], l_rs.at[s], xp)

    def adjoint(k, x, s):
        def part(b):
            return jnp.dot(x[s], op[:, cols(b)], preferred_element_type=F32)

        ps[k, s, 0] = part(1 - e)
        launch(("sib", k, s, 0), sib_copy(k, s, 0))
        cc[k, s, 0] = part(e)
        ps[k, s, 1] = part(2 + 1 - e)
        launch(("sib", k, s, 1), sib_copy(k, s, 1))
        for i in range(2):
            if i == 1:
                cc[k, s, 1] = part(2 + e)
            land("sib", k, s, i)
            c = cc[k, s, i] + pr[k, s, i]
            cb = c.astype(BF16)
            cs[k, s, i] = cb
            launch(("x", k, s, i), x_copy(k, s, i))
            cc[k, s, i] = c
            if k == 0:
                cl[s, i] = (c - cb.astype(F32)).astype(BF16)

    def gather(k, s, i):
        land("x", k, s, i)
        v = cc[k, s, i] + cr[k, s, i].astype(F32)
        vop[k, s, 2 * i + e] = v.astype(BF16)
        launch(("ag", k, s, i), ag_copy(k, s, i, 2 * i + e))
        cc[k, s, i] = v

    def transpose_operator():
        at = [lax.broadcasted_iota(jnp.int32, (256, 256), d) for d in range(2)]
        eye[...] = jnp.where(at[0] == at[1], 1.0, 0.0).astype(BF16)

        def go(b, c):
            for q in range(2):
                for part in range(2):
                    for n in range(2):
                        rows = slice(part * ROWS + n * 512, part * ROWS + (n + 1) * 512)
                        col = pl.multiple_of(b * BLK + q * 256, 256)
                        ot[b, part * BLK + q * 256 : part * BLK + (q + 1) * 256, n * 512 : (n + 1) * 512] = nt_dot(
                            eye[...], op[rows, pl.ds(col, 256)]
                        ).astype(BF16)
            return c

        lax.fori_loop(0, 4, go, 0)

    def forward_block(k, s, b, dst, first):
        v = vop[k, s, b]
        xc[:, 0:BLK] = v
        xc[0:64, BLK:] = -v[64:128]
        xc[64:128, BLK:] = v[0:64]
        for n in range(2):
            lo, hi = n * 512, (n + 1) * 512
            part = jnp.dot(xc[...], ot[b, :, lo:hi], preferred_element_type=F32)
            if first:
                dst[s, :, lo:hi] = part
            else:
                dst[s, :, lo:hi] += part

    def forward(k, s, i, dst):
        forward_block(k, s, 2 * i + e, dst, i == 0)
        land("ag", k, s, i)
        forward_block(k, s, 2 * i + 1 - e, dst, False)

    def operand(s):
        y = (yy[s] * TAU).astype(BF16)
        xy[s, :, 0:ROWS] = y
        xy[s, 0:64, ROWS:] = y[64:128]
        xy[s, 64:128, ROWS:] = -y[0:64]

    def ar_start(n, tile):
        ar_src[n] = tile
        ar1[n, 0] = tile

        for d in AR_NEAR:
            remote(ar_src.at[n], ar1.at[n, d], r_ss.at[n, 0], r_rs.at[n, 0], peer1(d)).start()
        ar_flying(n, 0, ar1)

    def ar_flying(n, stage, ref):
        part = ref.at[n, pl.ds(1, 15)]
        flying[("ar", n, stage), "send"] = local(part, part, r_ss.at[n, stage]).wait
        flying[("ar", n, stage), "recv"] = local(part, part, r_rs.at[n, stage]).wait

    def ar_middle(n):
        land("ar", n, 0)
        tile = jnp.sum(ar1[n], axis=0)
        ar_mid[n] = tile
        ar2[n, 0] = tile

        for d in AR_FAR:
            remote(ar_mid.at[n], ar2.at[n, d], r_ss.at[n, 1], r_rs.at[n, 1], peer2(d)).start()
        ar_flying(n, 1, ar2)

    def ar_end(n):
        land("ar", n, 1)
        return jnp.sum(jnp.sum(ar2[n], axis=0), axis=1, keepdims=True)

    def tile_of(rows):
        at = lax.broadcasted_iota(jnp.int32, (8, 128), 0)
        tile = jnp.zeros((8, 128), F32)
        for i, row in enumerate(rows):
            tile = jnp.where(at == i, row, tile)
        return tile

    def body():
        land("tb")
        dft(0)
        pl.semaphore_wait(barrier, FREQS - 1 + 12)
        a2a_send(0)
        dft(1)
        land("op")
        transpose_operator()
        a2a_send(1)

        zero = jnp.zeros((1, 128), F32)
        sum_u = zero
        for s in range(2):
            land("a2a", s)
            sum_u = sum_u + relayout(s)
            adjoint(0, xu, s)

        sum_v, sum_y, sum_yu = zero, zero, zero
        for s in range(2):
            for i in range(2):
                gather(0, s, i)
                forward(0, s, i, yy)
            operand(s)
            adjoint(1, xy, s)
            v = cc[0, s, h]
            sum_v = sum_v + lane_sums(v * v)
            sum_y = sum_y + lane_sums(yy[s] * yy[s])
            sum_yu = sum_yu + lane_sums(yy[s] * xu[s, :, 0:ROWS].astype(F32))
            if s == 0:
                ar_start(0, tile_of([sum_u, sum_v, sum_y]))
        ar_middle(0)

        sum_r, sum_rv, sum_g, sum_gy, sum_gu = zero, zero, zero, zero, zero
        for i in range(2):
            gather(1, 0, i)
            forward(1, 0, i, zz)
        gather(1, 1, 0)
        forward(1, 1, 0, zz)
        total = ar_end(0)
        s_u = total[0:1]
        kappa = total[2:3] / jnp.maximum(total[1:2], 1e-30) * TAU
        for s in range(2):
            zz[s] -= kappa * yy[s]
            if s == 1:
                gather(1, 1, 1)
                for t in range(2):
                    launch(("lo", t), lo_copy(t))
            v = cc[0, s, h]
            right = cc[1, s, h] - kappa * v
            sum_r = sum_r + lane_sums(right * right)
            sum_rv = sum_rv + lane_sums(right * v)
            if s == 1:
                forward(1, 1, 1, zz)
            y = yy[s]
            ahead = zz[s]
            sum_g = sum_g + lane_sums(ahead * ahead)
            sum_gy = sum_gy + lane_sums(ahead * y)
            sum_gu = sum_gu + lane_sums(ahead * xu[s, :, 0:ROWS].astype(F32))
        ar_start(1, tile_of([sum_v, sum_y, sum_yu, sum_r, sum_rv, sum_g, sum_gy, sum_gu]))
        ar_middle(1)
        total = ar_end(1)
        s_v, s_y, s_yu, s_r, s_rv, s_g, s_gy, s_gu = (total[i : i + 1] for i in range(8))
        beta0 = jnp.sqrt(s_u * (1.0 / SIGMA**2) + EPS)
        sb0 = beta0 * SIGMA
        alpha0_sq = s_v / (sb0 * sb0) + EPS
        alpha0 = jnp.sqrt(alpha0_sq)
        g0 = sb0 * alpha0
        s_left = jnp.maximum(s_y - alpha0_sq * (2.0 * s_yu - alpha0_sq * s_u), 0.0)
        beta1_sq = s_left / (g0 * g0) + EPS
        beta1 = jnp.sqrt(beta1_sq)
        k1 = (alpha0_sq + beta1_sq) * TAU
        delta = k1 - kappa
        s_r = jnp.maximum(s_r - delta * (2.0 * s_rv - delta * s_v), 0.0)
        s_gl = s_gy - alpha0_sq * s_gu - delta * (s_y - alpha0_sq * s_yu)
        s_g = jnp.maximum(s_g - delta * (2.0 * s_gy - delta * s_y), 0.0)
        g1s = g0 * beta1 * TAU
        alpha1_sq = s_r / (g1s * g1s) + EPS
        alpha1 = jnp.sqrt(alpha1_sq)
        g2s = g1s * alpha1
        a_sq = alpha1_sq * TAU
        s_left2 = jnp.maximum(s_g - a_sq * (2.0 * s_gl - a_sq * s_left), 0.0)
        beta2_sq = s_left2 / (g2s * g2s) + EPS

        rho1_sq = alpha0_sq + beta1_sq
        rho1 = jnp.sqrt(rho1_sq)
        cos1 = alpha0 / rho1
        sin1 = beta1 / rho1
        theta1 = sin1 * alpha1
        rhobar = cos1 * alpha1
        phi1 = cos1 * beta0
        phibar = sin1 * beta0
        rho2 = jnp.sqrt(rhobar * rhobar + beta2_sq)
        phi2 = (rhobar / rho2) * phibar
        y2 = -(phi2 / rho2)
        c_v = (phi1 / rho1 - y2 * (theta1 / rho1)) / g0
        c_r = y2 / g2s
        for s in range(2):
            land("lo", s)
            v = cc[0, s, h] + clr[s].astype(F32)
            right = cc[1, s, h] - k1 * v
            x = c_v * v + c_r * right
            for c in range(2):
                for t in range(4):
                    tmp[t, pl.ds(c * 128 + s, 64, stride=2), :] = x[
                        c * 64 : (c + 1) * 64, t * 128 : (t + 1) * 128
                    ]
        for c in range(2):
            for t in range(4):
                out_ref[pl.ds(t * 256 + c, 128, stride=2), :] = tmp[t, c * 128 : (c + 1) * 128, :].T

    body()
    for wait in flying.values():
        wait()


def per_device(table, traces, downgoing):
    vmem = pltpu.VMEM
    dma = pltpu.SemaphoreType.DMA
    scratch = [
        vmem((4 * FREQS, SAMPLES), BF16),
        vmem((2, ROWS, SAMPLES), BF16),
        vmem((2 * ROWS, COLS), BF16),
        vmem((FREQS * 16, 128), F32),
        vmem((FREQS * 16, 128), F32),
        vmem((FREQS, 32, 128), BF16),
        vmem((FREQS, 32, 128), BF16),
        vmem((2, M, 2 * ROWS), BF16),
        vmem((2, M, 2 * ROWS), BF16),
        vmem((2, 2, 2, M, BLK), F32),
        vmem((2, 2, 2, M, BLK), F32),
        vmem((2, 2, 2, M, BLK), F32),
        vmem((2, 2, 2, M, BLK), BF16),
        vmem((2, 2, 2, M, BLK), BF16),
        vmem((2, 2, M, BLK), BF16),
        vmem((2, M, BLK), BF16),
        vmem((2, 2, 4, M, BLK), BF16),
        vmem((M, 2 * BLK), BF16),
        vmem((256, 256), BF16),
        vmem((4, 2 * BLK, ROWS), BF16),
        vmem((2, M, ROWS), F32),
        vmem((2, M, ROWS), F32),
        vmem((4, 2 * M, 128), F32),
        vmem((2, 8, 128), F32),
        vmem((2, 16, 8, 128), F32),
        vmem((2, 8, 128), F32),
        vmem((2, 16, 8, 128), F32),
        dma, dma((2,)), dma,
        dma((2,)), dma((2,)),
        dma((2, 2, 2)), dma((2, 2, 2)),
        dma((2, 2, 2)), dma((2, 2, 2)),
        dma((2, 2, 2)), dma((2, 2, 2)),
        dma((2,)), dma((2,)),
        dma((2, 2)), dma((2, 2)),
    ]
    out = pl.pallas_call(
        kernel,
        out_shape=jax.ShapeDtypeStruct((2 * BLK, 128), F32),
        in_specs=[
            pl.BlockSpec(memory_space=pl.ANY),
            pl.BlockSpec(memory_space=pl.ANY),
            pl.BlockSpec(memory_space=pl.ANY),
        ],
        out_specs=pl.BlockSpec(memory_space=pltpu.VMEM),
        scratch_shapes=scratch,
        compiler_params=pltpu.CompilerParams(
            collective_id=0, has_side_effects=True, vmem_limit_bytes=63 * 2**20
        ),
        name="lsqr",
    )(table, traces, downgoing.reshape(2 * ROWS, COLS))
    return out.reshape(1, BLK, 2, 128)


def solution(mesh):
    table = dft_table()
    return jax.shard_map(
        lambda traces, downgoing: per_device(jnp.asarray(table), traces, downgoing),
        mesh=mesh,
        in_specs=(P("freq", "rcv", None), P("freq", None, "rcv", None)),
        out_specs=P("freq", "rcv", None, None),
        check_vma=False,
    )
```
